32 devices in a mesh: group: 4 (over y, core), seq: 2 (over x), rep: 4 (over z).
Axes of the slice: x: 2, y: 2, z: 4, core: 2. Of those that a mesh axis runs over, the one named last changes fastest.
Arguments:
- query_raw: bfloat16 [4, 4, 256, 3072], P('rep', 'group', 'seq'), may hold values from -1000 to 1000
- key_raw: bfloat16 [4, 4, 256, 3072], P('rep', 'group', 'seq'), may hold values from -1000 to 1000
- value_in: bfloat16 [4, 4, 256, 3072], P('rep', 'group', 'seq'), may hold values from -6 to 6
- out_cotangent: bfloat16 [4, 4, 256, 3072], P('rep', 'group', 'seq'), may hold values from -25 to 25
- query_gain: float32 [3072], replicated, may hold values from 0.5 to 1.5
- key_gain: float32 [3072], replicated, may hold values from 0.5 to 1.5
- attend_from: int32 [4, 4], P('rep', 'group'), may hold values from 0 to 3, as said below
Outputs:
- query_grad: bfloat16 [4, 4, 256, 3072], P('rep', 'group', 'seq')
- key_grad: bfloat16 [4, 4, 256, 3072], P('rep', 'group', 'seq')
- value_grad: bfloat16 [4, 4, 256, 3072], P('rep', 'group', 'seq')
- query_gain_grad: float32 [3072], P('rep')
- key_gain_grad: float32 [3072], P('rep')
The draws below stay inside these ranges and needn't reach their ends.
Inputs may be any that keep to these rules, and one draw needn't show every extreme that they name: For group c, max(0, c - 2) <= attend_from[b, c] <= c.
All inputs are finite; a program needn't handle non-finite values.
Results may differ from the reference program's by a relative error of at most 0.012.
The reference program's roundings to bfloat16 on the way count: a program that leaves them out, or rounds other values in their place, can miss the bound.
Values may be sent and summed in bfloat16 or wider, within the bound.
A program may use at most 128 MiB of HBM per device.

```python
import math
import jax
import jax.numpy as jnp
from jax import lax

HEADS = 24
HEAD_DIM = 128
PAST = 2
GROUP_LEN = 256
GROUPS = 4
CLIPS = 4
HD = 3072


def shared_parts(key):
    column_scale = jnp.exp(jax.random.uniform(jax.random.fold_in(key, 12), (HD,), jnp.float32, 0.0, math.log(10.0)))
    return column_scale


def row_scales(key):
    return jnp.exp(jax.random.uniform(key, (CLIPS, GROUPS, GROUP_LEN, 1), jnp.float32, 0.0, math.log(10.0)))


def draw_key_raw(key, part):
    column_scale = shared_parts(key)
    key = jax.random.fold_in(key, 2)
    shape = (CLIPS, GROUPS, GROUP_LEN, HD)
    row_scale = row_scales(jax.random.fold_in(key, 1))
    return (jax.random.normal(jax.random.fold_in(key, 2), shape, jnp.float32) * column_scale * row_scale).astype(jnp.bfloat16)


def draw_query_raw(key, part):
    column_scale = shared_parts(key)
    key = jax.random.fold_in(key, 3)
    shape = (CLIPS, GROUPS, GROUP_LEN, HD)
    row_scale = row_scales(jax.random.fold_in(key, 1))
    return (jax.random.normal(jax.random.fold_in(key, 2), shape, jnp.float32) * column_scale * row_scale).astype(jnp.bfloat16)


def draw_out_cotangent(key, part):
    key = jax.random.fold_in(key, 5)
    shape = (CLIPS, GROUPS, GROUP_LEN, HD)
    noise = jnp.clip(jax.random.normal(jax.random.fold_in(key, 1), shape, jnp.float32), -6.0, 6.0)
    clip_rise = 1.0 + 2.0 * jnp.arange(CLIPS, dtype=jnp.float32) / max(CLIPS - 1, 1)
    group_rise = 1.0 + 2.0 * jnp.arange(GROUPS, dtype=jnp.float32) / max(GROUPS - 1, 1)
    token_rise = 1.0 + 2.0 * jnp.arange(GROUP_LEN, dtype=jnp.float32) / max(GROUP_LEN - 1, 1)
    factor_all = clip_rise[:, None, None, None] * group_rise[None, :, None, None] * token_rise[None, None, :, None]
    return (0.15 * noise * factor_all).astype(jnp.bfloat16)


def draw_attend_from(key, part):
    key = jax.random.fold_in(key, 7)
    backward = jax.random.randint(key, (CLIPS, GROUPS), 0, PAST + 1)
    group_ids = jnp.arange(GROUPS, dtype=jnp.int32)[None, :]
    first_group = jnp.maximum(group_ids - backward, 0)
    first_group = first_group.at[0, GROUPS - 1].set(GROUPS - 1)
    first_group = first_group.at[1, GROUPS - 1].set(GROUPS - 1 - PAST)
    return first_group.astype(jnp.int32)


def shard_levels(rng, shape, pieces, least, top_value):
    gain, own = 1.0, jax.random.fold_in(rng, 6)
    for axis_at, blocks in pieces:
        steps = jnp.exp(jax.random.uniform(jax.random.fold_in(own, axis_at), (blocks,), jnp.float32, least / len(pieces), top_value / len(pieces)))
        gain = gain * jnp.repeat(steps, shape[axis_at] // blocks).reshape([-1 if axis == axis_at else 1 for axis in range(len(shape))])
    return gain


def centred(rng, dims, scale, limit, pieces=(), kind=jnp.bfloat16):
    array = jax.random.normal(rng, dims, jnp.float32) * scale
    if len(pieces) > 0:
        array = shard_levels(rng, dims, pieces, -0.22, 0.18) * array
    return jnp.clip(array, min=-limit, max=limit).astype(kind)


def setup_inputs(seed: int = 0) -> dict:
    splits = jax.random.split(jax.random.key(seed), 8)
    return {
        "query_raw": draw_query_raw(jax.random.fold_in(splits[7], 71), 0),
        "key_raw": draw_key_raw(jax.random.fold_in(splits[7], 71), 0),
        "value_in": centred(splits[2], (CLIPS, GROUPS, GROUP_LEN, HD), 1.0, 6.0, ((0, 4), (1, 4), (2, 2))),
        "out_cotangent": draw_out_cotangent(jax.random.fold_in(splits[7], 71), 0),
        "query_gain": jnp.clip(1.0 + 0.1 * jax.random.normal(splits[4], (HD,), jnp.float32), 0.5, 1.5),
        "key_gain": jnp.clip(1.0 + 0.1 * jax.random.normal(splits[5], (HD,), jnp.float32), 0.5, 1.5),
        "attend_from": draw_attend_from(jax.random.fold_in(splits[7], 71), 0),
    }


EPSILON = 1e-06

def normalize(row_values, gain_vec):
    values = row_values.astype(jnp.float32)
    inv_rms = lax.rsqrt(lax.optimization_barrier(jnp.mean(values * values, axis=-1, keepdims=True)) + EPSILON)
    return (values, inv_rms, (values * inv_rms * gain_vec).astype(jnp.bfloat16))

def denormalize(values, inv_rms, gain_vec, grad_low):
    upstream = grad_low.astype(jnp.float32)
    weighted = upstream * gain_vec
    inner_mean = lax.optimization_barrier(jnp.mean(values * weighted, axis=-1, keepdims=True))
    result = inv_rms * weighted - values * (inv_rms * inv_rms * inv_rms) * inner_mean
    gain_terms = lax.optimization_barrier(jnp.sum((upstream * values * inv_rms).reshape(-1, values.shape[-1]), axis=0))
    return (result.astype(jnp.bfloat16), gain_terms)

def head_grads(query_head, key_head, value_head, cot_head, visible, factor):
    scores = jnp.dot(query_head, key_head.T, preferred_element_type=jnp.float32) * factor
    scores = jnp.where(visible[None, :], scores, -1e+30)
    row_max = lax.optimization_barrier(jnp.max(scores, axis=1, keepdims=True))
    weights = jnp.exp(scores - row_max)
    probabilities = weights / lax.optimization_barrier(jnp.sum(weights, axis=1, keepdims=True))
    probs_low = probabilities.astype(jnp.bfloat16)
    dprobs = jnp.dot(cot_head, value_head.T, preferred_element_type=jnp.float32)
    row_delta = lax.optimization_barrier(jnp.sum(probabilities * dprobs, axis=1, keepdims=True))
    dscores = (probabilities * (dprobs - row_delta)).astype(jnp.bfloat16)
    query_part = jnp.dot(dscores, key_head, preferred_element_type=jnp.float32) * factor
    key_part = jnp.dot(dscores.T, query_head, preferred_element_type=jnp.float32) * factor
    value_part = jnp.dot(probs_low.T, cot_head, preferred_element_type=jnp.float32)
    return (query_part, key_part, value_part)

def reference(query_raw, key_raw, value_in, out_cotangent, query_gain, key_gain, attend_from):
    factor = HEAD_DIM ** (-0.5)
    window_len = PAST + 1
    zero_index = jnp.zeros((), jnp.int32)
    query_grads = []
    key_grads = []
    value_grads = []
    query_gain_grad = jnp.zeros((HD,), jnp.float32)
    key_gain_grad = jnp.zeros((HD,), jnp.float32)
    for clip_index in range(CLIPS):
        q_values, q_inv, q_normed = normalize(query_raw[clip_index], query_gain)
        k_values, k_inv, k_normed = normalize(key_raw[clip_index], key_gain)
        padding = jnp.zeros((PAST, GROUP_LEN, HD), jnp.bfloat16)
        keys_padded = jnp.concatenate([padding, k_normed], axis=0)
        values_padded = jnp.concatenate([padding, value_in[clip_index]], axis=0)
        cotangents = out_cotangent[clip_index]
        limits = attend_from[clip_index]

        def group_step(state_tuple, group_index):
            key_acc, value_acc = state_tuple
            corner = (group_index, zero_index, zero_index)
            sizes_win = (window_len, GROUP_LEN, HD)
            key_window = lax.dynamic_slice(keys_padded, corner, sizes_win).reshape(window_len * GROUP_LEN, HD)
            value_window = lax.dynamic_slice(values_padded, corner, sizes_win).reshape(window_len * GROUP_LEN, HD)
            key_owner = group_index - PAST + jnp.arange(window_len * GROUP_LEN, dtype=jnp.int32) // GROUP_LEN
            visible = key_owner >= limits[group_index]
            query_group = q_normed[group_index]
            cot_group = cotangents[group_index]

            def per_head(head_index):
                column_start = head_index * HEAD_DIM
                return head_grads(lax.dynamic_slice_in_dim(query_group, column_start, HEAD_DIM, 1), lax.dynamic_slice_in_dim(key_window, column_start, HEAD_DIM, 1), lax.dynamic_slice_in_dim(value_window, column_start, HEAD_DIM, 1), lax.dynamic_slice_in_dim(cot_group, column_start, HEAD_DIM, 1), visible, factor)
            query_part, key_part, value_part = lax.map(per_head, jnp.arange(HEADS, dtype=jnp.int32))
            query_rows = jnp.transpose(query_part, (1, 0, 2)).reshape(GROUP_LEN, HD)
            key_rows = jnp.transpose(key_part, (1, 0, 2)).reshape(window_len, GROUP_LEN, HD)
            value_rows = jnp.transpose(value_part, (1, 0, 2)).reshape(window_len, GROUP_LEN, HD)
            key_acc = lax.dynamic_update_slice(key_acc, lax.dynamic_slice(key_acc, corner, sizes_win) + key_rows, corner)
            value_acc = lax.dynamic_update_slice(value_acc, lax.dynamic_slice(value_acc, corner, sizes_win) + value_rows, corner)
            return ((key_acc, value_acc), query_rows.astype(jnp.bfloat16))
        initial = (jnp.zeros((PAST + GROUPS, GROUP_LEN, HD), jnp.float32), jnp.zeros((PAST + GROUPS, GROUP_LEN, HD), jnp.float32))
        (key_acc, value_acc), query_low = lax.scan(group_step, initial, jnp.arange(GROUPS, dtype=jnp.int32))
        key_low = key_acc[PAST:].astype(jnp.bfloat16)
        value_low = value_acc[PAST:].astype(jnp.bfloat16)
        query_result, query_terms = denormalize(q_values, q_inv, query_gain, query_low)
        key_result, key_terms = denormalize(k_values, k_inv, key_gain, key_low)
        query_grads.append(query_result)
        key_grads.append(key_result)
        value_grads.append(value_low)
        query_gain_grad = query_gain_grad + query_terms
        key_gain_grad = key_gain_grad + key_terms
    return (jnp.stack(query_grads), jnp.stack(key_grads), jnp.stack(value_grads), query_gain_grad, key_gain_grad)
```

```python
import functools

import jax
import jax.numpy as jnp
from jax import lax
from jax.experimental import pallas as pl
from jax.experimental.pallas import tpu as pltpu
from jax.sharding import PartitionSpec as P

HEAD_DIM = 128
PAST = 2


EPSILON = 1e-06


def from_behind(block, axis, distance):
    devices = range(lax.axis_size(axis))
    route = [(i - distance, i) for i in devices if i - distance in devices]
    return lax.ppermute(block, axis, route)


def normalize(row_values, gain_vec):
    values = row_values.astype(jnp.float32)
    inv_rms = lax.rsqrt(jnp.mean(values * values, axis=-1, keepdims=True) + EPSILON)
    return (values, inv_rms, (values * inv_rms * gain_vec).astype(jnp.bfloat16))


def denormalize(values, inv_rms, gain_vec, grad_low):
    upstream = grad_low.astype(jnp.float32)
    weighted = upstream * gain_vec
    inner_mean = jnp.mean(values * weighted, axis=-1, keepdims=True)
    result = inv_rms * weighted - values * (inv_rms * inv_rms * inv_rms) * inner_mean
    gain_terms = jnp.sum(upstream * values * inv_rms, axis=0)
    return (result.astype(jnp.bfloat16), gain_terms)


def head_pass(query_head, key_head, value_head, cot_head, visible, factor):
    scores = jnp.dot(query_head, key_head.T, preferred_element_type=jnp.float32) * factor
    scores = jnp.where(visible[None, :], scores, -1e30)
    row_max = jnp.max(scores, axis=1, keepdims=True)
    weights = jnp.exp(scores - row_max)
    row_total = jnp.sum(weights, axis=1, keepdims=True)
    probabilities = weights / row_total
    probs_low = probabilities.astype(jnp.bfloat16)
    dprobs = jnp.dot(cot_head, value_head.T, preferred_element_type=jnp.float32)
    row_delta = jnp.sum(probabilities * dprobs, axis=1, keepdims=True)
    dscores = (probabilities * (dprobs - row_delta)).astype(jnp.bfloat16)
    query_part = jnp.dot(dscores, key_head, preferred_element_type=jnp.float32) * factor
    key_part = jnp.dot(dscores.T, query_head, preferred_element_type=jnp.float32) * factor
    value_part = jnp.dot(probs_low.T, cot_head, preferred_element_type=jnp.float32)
    return (query_part, key_part, value_part, row_max[:, 0], row_total[:, 0], row_delta[:, 0])


def pass_forward(kv_pair, hop_count):
    return from_behind(kv_pair, "group", hop_count)


def pass_back(cotangent_pair, hop_count):
    return from_behind(cotangent_pair, "group", hop_count)


MESH = pl.DeviceIdType.MESH
ROWS = 16
NT = (((1,), (1,)), ((), ()))


def dot(left, right, dims=(((1,), (0,)), ((), ()))):
    return lax.dot_general(left, right, dims, preferred_element_type=jnp.float32)


def head_kernel(
    sizes,
    attend_ref, q_hbm, k_hbm, v_hbm, c_hbm, q_gain, k_gain,
    q_out, k_out, v_out, q_gain_out, k_gain_out,
    raw, normed, inv, heads, grads, back, first, acc, terms, gathered,
    raw_sem, send_sem, recv_sem, own_sem, back_send, back_recv, back_own,
    first_send, first_recv, terms_send, terms_recv,
):
    groups, seqs, reps, tokens, width, per_owner = sizes
    owners = groups * seqs
    group_len = seqs * tokens
    own_width = per_owner * HEAD_DIM
    per_rep = owners // reps
    group, seq, rep = lax.axis_index("group"), lax.axis_index("seq"), lax.axis_index("rep")
    me = group * seqs + seq
    factor = HEAD_DIM ** (-0.5)

    loads = []
    for which, source in enumerate((q_hbm, k_hbm)):
        load = pltpu.make_async_copy(source, raw.at[which], raw_sem.at[which])
        load.start()
        loads.append(load)

    barrier = pltpu.get_barrier_semaphore()
    devices = owners * reps
    flat = me * reps + rep

    def greet(step, carry):
        other = lax.rem(flat + step, devices)
        place = {
            "group": other // (seqs * reps),
            "seq": lax.rem(other // reps, seqs),
            "rep": lax.rem(other, reps),
        }
        pl.semaphore_signal(barrier, inc=1, device_id=place, device_id_type=MESH)
        return carry

    lax.fori_loop(1, devices, greet, 0)

    def partner(step):
        other = lax.rem(me + step, owners)
        return other, {"group": other // seqs, "seq": lax.rem(other, seqs)}

    my_rows = pl.ds(pl.multiple_of(me * tokens, tokens), tokens)

    def columns(owner, head):
        return pl.ds(pl.multiple_of(owner * own_width + head * HEAD_DIM, HEAD_DIM), HEAD_DIM)

    def send_heads(which, source, head):
        for step in range(1, owners):
            other, place = partner(step)
            pltpu.make_async_remote_copy(
                src_ref=source.at[:, columns(other, head)],
                dst_ref=heads.at[which, head, my_rows],
                send_sem=send_sem.at[which, head],
                recv_sem=recv_sem.at[which, head],
                device_id=place,
                device_id_type=MESH,
            ).start()
        pltpu.make_async_copy(
            source.at[:, columns(me, head)], heads.at[which, head, my_rows], recv_sem.at[which, head]
        ).start()

    def normalize_rows(which, gain_ref):
        def step(index, carry):
            rows = pl.ds(pl.multiple_of(index * ROWS, ROWS), ROWS)
            values = raw[which, rows, :].astype(jnp.float32)
            scale = lax.rsqrt(jnp.mean(values * values, axis=-1, keepdims=True) + EPSILON)
            inv[which, rows, :] = scale
            normed[which, rows, :] = (values * scale * gain_ref[...]).astype(jnp.bfloat16)
            return carry

        lax.fori_loop(0, tokens // ROWS, step, 0)

    first[me] = jnp.full(first.shape[1:], attend_ref[0, 0].astype(jnp.float32))
    pl.semaphore_wait(barrier, devices - 1)
    for step in range(1, owners):
        other, place = partner(step)
        pltpu.make_async_remote_copy(
            src_ref=first.at[me],
            dst_ref=first.at[me],
            send_sem=first_send,
            recv_sem=first_recv,
            device_id=place,
            device_id_type=MESH,
        ).start()
    send_heads(2, v_hbm, 0)
    send_heads(3, c_hbm, 0)
    loads[0].wait()
    normalize_rows(0, q_gain)
    send_heads(0, normed.at[0], 0)
    loads[1].wait()
    normalize_rows(1, k_gain)
    send_heads(1, normed.at[1], 0)

    def send_rest(head, carry):
        for which, source in ((0, normed.at[0]), (1, normed.at[1]), (2, v_hbm), (3, c_hbm)):
            send_heads(which, source, head)
        return carry

    lax.fori_loop(1, per_owner, send_rest, 0)

    terms[...] = jnp.zeros(terms.shape, jnp.float32)
    few = first.at[pl.ds(0, owners - 1)]
    pltpu.make_async_copy(few, few, first_recv).wait()

    def one_head(head, carry):
        for which in range(4):
            whole = heads.at[which, head]
            pltpu.make_async_copy(whole, whole, recv_sem.at[which, head]).wait()

        def block(which, index):
            return heads[which, head, index * group_len : (index + 1) * group_len, :]

        turned = [jnp.transpose(block(1, index)) for index in range(groups)]
        q_terms = jnp.zeros((1, HEAD_DIM), jnp.float32)
        k_terms = jnp.zeros((1, HEAD_DIM), jnp.float32)
        for group_at in range(groups):
            low = max(0, group_at - PAST)
            window = range(low, group_at + 1)
            q_block, c_block = block(0, group_at), block(3, group_at)
            first_row = first[group_at * seqs, 0:1, :]
            scores = []
            for index in window:
                score = dot(block(1, index), q_block, NT) * factor
                if index < group_at:
                    score = score + jnp.where(first_row > index, -1e30, 0.0)
                scores.append(score)
            top = functools.reduce(
                jnp.maximum, [jnp.max(score, axis=0, keepdims=True) for score in scores]
            )
            weights = [jnp.exp(score - top) for score in scores]
            total = sum(jnp.sum(weight, axis=0, keepdims=True) for weight in weights)
            share = 1.0 / total
            probs = [weight * share for weight in weights]
            dprobs = [dot(block(2, index), c_block, NT) for index in window]
            delta = sum(
                jnp.sum(prob * dprob, axis=0, keepdims=True) for prob, dprob in zip(probs, dprobs)
            )
            q_turned = jnp.zeros((HEAD_DIM, group_len), jnp.float32)
            for index, prob, dprob in zip(window, probs, dprobs):
                rows = slice(index * group_len, (index + 1) * group_len)
                dscore = (prob * (dprob - delta)).astype(jnp.bfloat16)
                k_part = dot(dscore, q_block)
                v_part = dot(prob.astype(jnp.bfloat16), c_block)
                if index < group_at:
                    k_part = k_part + acc[0, rows, :]
                    v_part = v_part + acc[1, rows, :]
                if group_at == min(index + PAST, groups - 1):
                    k_low = (k_part * factor).astype(jnp.bfloat16)
                    grads[1, head, rows, :] = k_low
                    grads[2, head, rows, :] = v_part.astype(jnp.bfloat16)
                    k_terms = k_terms + jnp.sum(
                        k_low.astype(jnp.float32) * block(1, index).astype(jnp.float32),
                        axis=0,
                        keepdims=True,
                    )
                else:
                    acc[0, rows, :] = k_part
                    acc[1, rows, :] = v_part
                q_turned = q_turned + dot(turned[index], dscore)
            q_low = (jnp.transpose(q_turned) * factor).astype(jnp.bfloat16)
            grads[0, head, group_at * group_len : (group_at + 1) * group_len, :] = q_low
            q_terms = q_terms + jnp.sum(
                q_low.astype(jnp.float32) * q_block.astype(jnp.float32), axis=0, keepdims=True
            )
        terms[head, 0:1, :] = q_terms / q_gain[:, columns(me, head)]
        terms[head, 1:2, :] = k_terms / k_gain[:, columns(me, head)]
        for which, landing in ((0, back.at[0]), (1, back.at[1]), (2, v_out)):
            for step in range(1, owners):
                other, place = partner(step)
                pltpu.make_async_remote_copy(
                    src_ref=grads.at[which, head, pl.ds(pl.multiple_of(other * tokens, tokens), tokens)],
                    dst_ref=landing.at[:, columns(me, head)],
                    send_sem=back_send.at[which],
                    recv_sem=back_recv.at[which],
                    device_id=place,
                    device_id_type=MESH,
                ).start()
            pltpu.make_async_copy(
                grads.at[which, head, my_rows], landing.at[:, columns(me, head)], back_recv.at[which]
            ).start()
        return carry

    lax.fori_loop(0, per_owner, one_head, 0)

    target_rep = me // per_rep
    slot = rep * per_rep + lax.rem(me, per_rep)

    def send_terms(place):
        pltpu.make_async_remote_copy(
            src_ref=terms,
            dst_ref=gathered.at[slot],
            send_sem=terms_send,
            recv_sem=terms_recv,
            device_id={**place, "rep": target_rep},
            device_id_type=MESH,
        ).start()

    for step in range(1, owners):
        send_terms(partner(step)[1])

    @pl.when(rep != target_rep)
    def _():
        send_terms(partner(0)[1])

    @pl.when(rep == target_rep)
    def _():
        pltpu.make_async_copy(terms, gathered.at[slot], terms_recv).start()

    def denormalize_rows(which, gain_ref, out_ref):
        def step(index, carry):
            rows = pl.ds(pl.multiple_of(index * ROWS, ROWS), ROWS)
            values = raw[which, rows, :].astype(jnp.float32)
            scale = inv[which, rows, :]
            weighted = back[which, rows, :].astype(jnp.float32) * gain_ref[...]
            inner = jnp.mean(values * weighted, axis=-1, keepdims=True)
            result = scale * weighted - values * (scale * scale * scale * inner)
            out_ref[rows, :] = result.astype(jnp.bfloat16)
            return carry

        lax.fori_loop(0, tokens // ROWS, step, 0)

    for which, gain_ref, out_ref in ((0, q_gain, q_out), (1, k_gain, k_out)):
        pltpu.make_async_copy(back.at[which], back.at[which], back_recv.at[which]).wait()
        denormalize_rows(which, gain_ref, out_ref)

    pltpu.make_async_copy(gathered, gathered, terms_recv).wait()
    for sub in range(per_rep):
        for head in range(per_owner):
            lanes = slice((sub * per_owner + head) * HEAD_DIM, (sub * per_owner + head + 1) * HEAD_DIM)
            sums = sum(gathered[clip * per_rep + sub, head] for clip in range(reps))
            q_gain_out[:, lanes] = sums[0:1]
            k_gain_out[:, lanes] = sums[1:2]
    pltpu.make_async_copy(v_out, v_out, back_recv.at[2]).wait()

    pltpu.make_async_copy(few, few, first_send).wait()
    for which in range(4):
        for head in range(per_owner):
            sent = heads.at[which, head, pl.ds(0, (owners - 1) * tokens)]
            pltpu.make_async_copy(sent, sent, send_sem.at[which, head]).wait()
    for which in range(3):
        sent = grads.at[which, :, pl.ds(0, (owners - 1) * tokens)]
        pltpu.make_async_copy(sent, sent, back_send.at[which]).wait()
    sent = gathered.at[pl.ds(0, owners - 1)]
    pltpu.make_async_copy(sent, sent, terms_send).wait()

    @pl.when(rep != target_rep)
    def _():
        pltpu.make_async_copy(terms, terms, terms_send).wait()


def head_body(query_raw, key_raw, value_in, out_cotangent, query_gain, key_gain, attend_from):
    groups, seqs, reps = (lax.axis_size(name) for name in ("group", "seq", "rep"))
    tokens, width = query_raw.shape[2:]
    owners = groups * seqs
    per_owner = width // HEAD_DIM // owners
    group_len = seqs * tokens
    clip_len = owners * tokens
    low = jnp.bfloat16
    rows = jax.ShapeDtypeStruct((tokens, width), low)
    gain_rows = jax.ShapeDtypeStruct((1, width // reps), jnp.float32)
    vmem = pl.BlockSpec(memory_space=pltpu.VMEM)
    hbm = pl.BlockSpec(memory_space=pl.ANY)
    dma = pltpu.SemaphoreType.DMA
    sizes = (groups, seqs, reps, tokens, width, per_owner)
    q_grad, k_grad, v_grad, q_gain_grad, k_gain_grad = pl.pallas_call(
        functools.partial(head_kernel, sizes),
        out_shape=(rows, rows, rows, gain_rows, gain_rows),
        in_specs=[pl.BlockSpec(memory_space=pltpu.SMEM)] + [hbm] * 4 + [vmem] * 2,
        out_specs=(vmem,) * 5,
        scratch_shapes=[
            pltpu.VMEM((2, tokens, width), low),
            pltpu.VMEM((2, tokens, width), low),
            pltpu.VMEM((2, tokens, 1), jnp.float32),
            pltpu.VMEM((4, per_owner, clip_len, HEAD_DIM), low),
            pltpu.VMEM((3, per_owner, clip_len, HEAD_DIM), low),
            pltpu.VMEM((2, tokens, width), low),
            pltpu.VMEM((owners, 8, group_len), jnp.float32),
            pltpu.VMEM((2, clip_len, HEAD_DIM), jnp.float32),
            pltpu.VMEM((per_owner, 8, HEAD_DIM), jnp.float32),
            pltpu.VMEM((owners, per_owner, 8, HEAD_DIM), jnp.float32),
            dma((2,)),
            dma((4, per_owner)),
            dma((4, per_owner)),
            dma,
            dma((3,)),
            dma((3,)),
            dma,
            dma,
            dma,
            dma,
            dma,
        ],
        compiler_params=pltpu.CompilerParams(
            collective_id=0, has_side_effects=True, vmem_limit_bytes=48 * 1024 * 1024
        ),
    )(
        attend_from,
        query_raw.reshape(tokens, width),
        key_raw.reshape(tokens, width),
        value_in.reshape(tokens, width),
        out_cotangent.reshape(tokens, width),
        query_gain.reshape(1, width),
        key_gain.reshape(1, width),
    )
    return (
        q_grad.reshape(query_raw.shape),
        k_grad.reshape(key_raw.shape),
        v_grad.reshape(value_in.shape),
        q_gain_grad.reshape(-1),
        k_gain_grad.reshape(-1),
    )


def ring_body(query_raw, key_raw, value_in, out_cotangent, query_gain, key_gain, attend_from):
    tok_rows = query_raw.shape[2]
    feature_width = query_raw.shape[3]
    q_values, q_inv, q_normed = normalize(query_raw.reshape(tok_rows, feature_width), query_gain)
    k_values, k_inv, k_normed = normalize(key_raw.reshape(tok_rows, feature_width), key_gain)
    heads_q, heads_k, heads_v, heads_cot = (
        lax.all_to_all(q_normed, "seq", split_axis=1, concat_axis=0, tiled=True),
        lax.all_to_all(k_normed, "seq", split_axis=1, concat_axis=0, tiled=True),
        lax.all_to_all(
            value_in.reshape(tok_rows, feature_width),
            "seq",
            split_axis=1,
            concat_axis=0,
            tiled=True,
        ),
        lax.all_to_all(
            out_cotangent.reshape(tok_rows, feature_width),
            "seq",
            split_axis=1,
            concat_axis=0,
            tiled=True,
        ),
    )
    group_len = heads_q.shape[0]
    head_width = heads_q.shape[1]
    window_len = PAST + 1
    own_pair = jnp.stack((heads_k, heads_v))
    earlier = []
    current = own_pair
    for hop_count in range(PAST):
        current = pass_forward(current, 1)
        earlier.insert(0, current)
    stacked = jnp.concatenate(earlier + [own_pair], axis=1)
    key_window = stacked[0]
    value_window = stacked[1]
    group_index = lax.axis_index("group")
    key_owner = (
        group_index - PAST + jnp.arange(window_len * group_len, dtype=jnp.int32) // group_len
    )
    visible = key_owner >= attend_from[0, 0]
    factor = HEAD_DIM ** (-0.5)
    query_block = 512 if group_len % 512 == 0 else group_len
    count_heads = head_width // HEAD_DIM
    key_rows_count = window_len * group_len

    def one_head(head_index, state_tuple):
        query_acc, key_acc, value_acc, max_acc, total_acc, delta_acc = state_tuple
        column_start = head_index * HEAD_DIM
        q_head = lax.dynamic_slice_in_dim(heads_q, column_start, HEAD_DIM, 1)
        cot_head = lax.dynamic_slice_in_dim(heads_cot, column_start, HEAD_DIM, 1)
        key_head = lax.dynamic_slice_in_dim(key_window, column_start, HEAD_DIM, 1)
        value_head = lax.dynamic_slice_in_dim(value_window, column_start, HEAD_DIM, 1)
        key_sum = jnp.zeros((key_rows_count, HEAD_DIM), jnp.float32)
        value_sum = jnp.zeros((key_rows_count, HEAD_DIM), jnp.float32)
        query_rows = []
        max_rows = []
        total_rows = []
        delta_rows = []
        for row_start in range(0, group_len, query_block):
            query_part, key_part, value_part, row_max, row_total, row_delta = head_pass(
                q_head[row_start : row_start + query_block],
                key_head,
                value_head,
                cot_head[row_start : row_start + query_block],
                visible,
                factor,
            )
            query_rows.append(query_part)
            max_rows.append(row_max)
            total_rows.append(row_total)
            delta_rows.append(row_delta)
            key_sum = key_sum + key_part
            value_sum = value_sum + value_part
        query_acc = lax.dynamic_update_slice_in_dim(
            query_acc, jnp.concatenate(query_rows, axis=0), column_start, 1
        )
        key_acc = lax.dynamic_update_slice_in_dim(key_acc, key_sum, column_start, 1)
        value_acc = lax.dynamic_update_slice_in_dim(value_acc, value_sum, column_start, 1)
        max_acc = lax.dynamic_update_slice_in_dim(
            max_acc, jnp.concatenate(max_rows)[:, None], head_index, 1
        )
        total_acc = lax.dynamic_update_slice_in_dim(
            total_acc, jnp.concatenate(total_rows)[:, None], head_index, 1
        )
        delta_acc = lax.dynamic_update_slice_in_dim(
            delta_acc, jnp.concatenate(delta_rows)[:, None], head_index, 1
        )
        return (query_acc, key_acc, value_acc, max_acc, total_acc, delta_acc)

    initial = (
        jnp.zeros((group_len, head_width), jnp.float32),
        jnp.zeros((key_rows_count, head_width), jnp.float32),
        jnp.zeros((key_rows_count, head_width), jnp.float32),
        jnp.zeros((group_len, count_heads), jnp.float32),
        jnp.zeros((group_len, count_heads), jnp.float32),
        jnp.zeros((group_len, count_heads), jnp.float32),
    )
    query_acc, key_acc, value_acc, max_all, total_all, delta_all = lax.fori_loop(
        0, count_heads, one_head, initial
    )
    cotangent_pair = jnp.stack((key_acc, value_acc))
    own_total = cotangent_pair[:, 0:group_len]
    for hop_count in range(1, PAST + 1):
        lower_row = hop_count * group_len
        own_total = pass_back(own_total, -1) + cotangent_pair[:, lower_row : lower_row + group_len]
    query_heads = query_acc.astype(jnp.bfloat16)
    key_heads = own_total[0].astype(jnp.bfloat16)
    value_heads = own_total[1].astype(jnp.bfloat16)
    token_q, token_k, token_v = (
        lax.all_to_all(query_heads, "seq", split_axis=0, concat_axis=1, tiled=True),
        lax.all_to_all(key_heads, "seq", split_axis=0, concat_axis=1, tiled=True),
        lax.all_to_all(value_heads, "seq", split_axis=0, concat_axis=1, tiled=True),
    )
    query_grad, query_terms = denormalize(q_values, q_inv, query_gain, token_q)
    key_grad, key_terms = denormalize(k_values, k_inv, key_gain, token_k)
    query_total, key_total_gain = lax.psum((query_terms, key_terms), ("group", "seq", "rep"))
    rep_width = feature_width // lax.axis_size("rep")
    offset = lax.axis_index("rep") * rep_width
    return (
        query_grad.reshape(query_raw.shape),
        key_grad.reshape(key_raw.shape),
        token_v.reshape(value_in.shape),
        lax.dynamic_slice_in_dim(query_total, offset, rep_width),
        lax.dynamic_slice_in_dim(key_total_gain, offset, rep_width),
    )


def body(*arrays):
    tokens, width = arrays[0].shape[2:]
    owners = lax.axis_size("group") * lax.axis_size("seq")
    heads = width // HEAD_DIM
    even = heads % owners == 0 and owners % lax.axis_size("rep") == 0
    if even and tokens * owners * heads <= 32768 and tokens % 16 == 0:
        return head_body(*arrays)
    return ring_body(*arrays)


def solution(mesh):
    placed = (
        P("rep", "group", "seq", None),
        P("rep", "group", "seq", None),
        P("rep", "group", "seq", None),
        P("rep", "group", "seq", None),
        P(),
        P(),
        P("rep", "group"),
    )
    return jax.shard_map(
        body,
        mesh=mesh,
        in_specs=placed,
        out_specs=(
            P("rep", "group", "seq", None),
            P("rep", "group", "seq", None),
            P("rep", "group", "seq", None),
            P("rep"),
            P("rep"),
        ),
        check_vma=False,
    )
```

```python
import functools

import jax
import jax.numpy as jnp
from jax import lax
from jax.experimental import pallas as pl
from jax.experimental.pallas import tpu as pltpu
from jax.sharding import PartitionSpec as P

HEAD_DIM = 128
PAST = 2


EPSILON = 1e-06


def from_behind(block, axis, distance):
    devices = range(lax.axis_size(axis))
    route = [(i - distance, i) for i in devices if i - distance in devices]
    return lax.ppermute(block, axis, route)


def normalize(row_values, gain_vec):
    values = row_values.astype(jnp.float32)
    inv_rms = lax.rsqrt(jnp.mean(values * values, axis=-1, keepdims=True) + EPSILON)
    return (values, inv_rms, (values * inv_rms * gain_vec).astype(jnp.bfloat16))


def denormalize(values, inv_rms, gain_vec, grad_low):
    upstream = grad_low.astype(jnp.float32)
    weighted = upstream * gain_vec
    inner_mean = jnp.mean(values * weighted, axis=-1, keepdims=True)
    result = inv_rms * weighted - values * (inv_rms * inv_rms * inv_rms) * inner_mean
    gain_terms = jnp.sum(upstream * values * inv_rms, axis=0)
    return (result.astype(jnp.bfloat16), gain_terms)


def head_pass(query_head, key_head, value_head, cot_head, visible, factor):
    scores = jnp.dot(query_head, key_head.T, preferred_element_type=jnp.float32) * factor
    scores = jnp.where(visible[None, :], scores, -1e30)
    row_max = jnp.max(scores, axis=1, keepdims=True)
    weights = jnp.exp(scores - row_max)
    row_total = jnp.sum(weights, axis=1, keepdims=True)
    probabilities = weights / row_total
    probs_low = probabilities.astype(jnp.bfloat16)
    dprobs = jnp.dot(cot_head, value_head.T, preferred_element_type=jnp.float32)
    row_delta = jnp.sum(probabilities * dprobs, axis=1, keepdims=True)
    dscores = (probabilities * (dprobs - row_delta)).astype(jnp.bfloat16)
    query_part = jnp.dot(dscores, key_head, preferred_element_type=jnp.float32) * factor
    key_part = jnp.dot(dscores.T, query_head, preferred_element_type=jnp.float32) * factor
    value_part = jnp.dot(probs_low.T, cot_head, preferred_element_type=jnp.float32)
    return (query_part, key_part, value_part, row_max[:, 0], row_total[:, 0], row_delta[:, 0])


def pass_forward(kv_pair, hop_count):
    return from_behind(kv_pair, "group", hop_count)


def pass_back(cotangent_pair, hop_count):
    return from_behind(cotangent_pair, "group", hop_count)


MESH = pl.DeviceIdType.MESH
ROWS = 16
STORE_PARTS = 4
NT = (((1,), (1,)), ((), ()))


def dot(left, right, dims=(((1,), (0,)), ((), ()))):
    return lax.dot_general(left, right, dims, preferred_element_type=jnp.float32)


def head_kernel(
    sizes,
    attend_ref, q_hbm, k_hbm, v_hbm, c_hbm, q_gain, k_gain,
    q_out, k_out, v_out, q_gain_out, k_gain_out,
    raw, normed, inv, heads, grads, back, first, acc, terms, gathered,
    raw_sem, send_sem, recv_sem, back_send, back_recv,
    first_send, first_recv, terms_send, terms_recv,
):
    groups, seqs, reps, tokens, width, per_owner = sizes
    owners = groups * seqs
    group_len = seqs * tokens
    own_width = per_owner * HEAD_DIM
    per_rep = owners // reps
    group, seq, rep = lax.axis_index("group"), lax.axis_index("seq"), lax.axis_index("rep")
    me = group * seqs + seq
    factor = HEAD_DIM ** (-0.5)

    loads = []
    for which, source in enumerate((q_hbm, k_hbm)):
        load = pltpu.make_async_copy(source, raw.at[which], raw_sem.at[which])
        load.start()
        loads.append(load)

    barrier = pltpu.get_barrier_semaphore()
    devices = owners * reps
    flat = me * reps + rep

    def greet(step, carry):
        other = lax.rem(flat + step, devices)
        place = {
            "group": other // (seqs * reps),
            "seq": lax.rem(other // reps, seqs),
            "rep": lax.rem(other, reps),
        }
        pl.semaphore_signal(barrier, inc=1, device_id=place, device_id_type=MESH)
        return carry

    lax.fori_loop(1, devices, greet, 0)

    def partner(step):
        other = lax.rem(me + step, owners)
        return other, {"group": other // seqs, "seq": lax.rem(other, seqs)}

    my_rows = pl.ds(pl.multiple_of(me * tokens, tokens), tokens)

    def columns(owner, head):
        return pl.ds(pl.multiple_of(owner * own_width + head * HEAD_DIM, HEAD_DIM), HEAD_DIM)

    def send_heads(which, source, head):
        for step in range(1, owners):
            other, place = partner(step)
            pltpu.make_async_remote_copy(
                src_ref=source.at[:, columns(other, head)],
                dst_ref=heads.at[which, head, my_rows],
                send_sem=send_sem.at[which, head],
                recv_sem=recv_sem.at[which, head],
                device_id=place,
                device_id_type=MESH,
            ).start()
        pltpu.make_async_copy(
            source.at[:, columns(me, head)], heads.at[which, head, my_rows], recv_sem.at[which, head]
        ).start()

    def normalize_rows(which, gain_ref):
        def step(index, carry):
            rows = pl.ds(pl.multiple_of(index * ROWS, ROWS), ROWS)
            values = raw[which, rows, :].astype(jnp.float32)
            scale = lax.rsqrt(jnp.mean(values * values, axis=-1, keepdims=True) + EPSILON)
            inv[which, rows, :] = scale
            normed[which, rows, :] = (values * scale * gain_ref[...]).astype(jnp.bfloat16)
            return carry

        lax.fori_loop(0, tokens // ROWS, step, 0)

    first[me] = jnp.full(first.shape[1:], attend_ref[0, 0].astype(jnp.float32))
    pl.semaphore_wait(barrier, devices - 1)
    for step in range(1, owners):
        other, place = partner(step)
        pltpu.make_async_remote_copy(
            src_ref=first.at[me],
            dst_ref=first.at[me],
            send_sem=first_send,
            recv_sem=first_recv,
            device_id=place,
            device_id_type=MESH,
        ).start()
    send_heads(2, v_hbm, 0)
    send_heads(3, c_hbm, 0)
    loads[0].wait()
    normalize_rows(0, q_gain)
    send_heads(0, normed.at[0], 0)
    loads[1].wait()
    normalize_rows(1, k_gain)
    send_heads(1, normed.at[1], 0)

    def send_rest(head, carry):
        for which, source in ((0, normed.at[0]), (1, normed.at[1]), (2, v_hbm), (3, c_hbm)):
            send_heads(which, source, head)
        return carry

    lax.fori_loop(1, per_owner, send_rest, 0)

    terms[...] = jnp.zeros(terms.shape, jnp.float32)
    few = first.at[pl.ds(0, owners - 1)]
    pltpu.make_async_copy(few, few, first_recv).wait()

    def one_head(head, carry):
        for which in range(4):
            whole = heads.at[which, head]
            pltpu.make_async_copy(whole, whole, recv_sem.at[which, head]).wait()

        def block(which, index):
            return heads[which, head, index * group_len : (index + 1) * group_len, :]

        turned = [jnp.transpose(block(1, index)) for index in range(groups)]
        q_terms = jnp.zeros((1, HEAD_DIM), jnp.float32)
        k_terms = jnp.zeros((1, HEAD_DIM), jnp.float32)
        for group_at in range(groups):
            low = max(0, group_at - PAST)
            window = range(low, group_at + 1)
            q_block, c_block = block(0, group_at), block(3, group_at)
            first_row = first[group_at * seqs, 0:1, :]
            scores = []
            for index in window:
                score = dot(block(1, index), q_block, NT) * factor
                if index < group_at:
                    score = score + jnp.where(first_row > index, -1e30, 0.0)
                scores.append(score)
            top = functools.reduce(
                jnp.maximum, [jnp.max(score, axis=0, keepdims=True) for score in scores]
            )
            weights = [jnp.exp(score - top) for score in scores]
            total = sum(jnp.sum(weight, axis=0, keepdims=True) for weight in weights)
            share = 1.0 / total
            probs = [weight * share for weight in weights]
            dprobs = [dot(block(2, index), c_block, NT) for index in window]
            delta = sum(
                jnp.sum(prob * dprob, axis=0, keepdims=True) for prob, dprob in zip(probs, dprobs)
            )
            q_turned = jnp.zeros((HEAD_DIM, group_len), jnp.float32)
            for index, prob, dprob in zip(window, probs, dprobs):
                rows = slice(index * group_len, (index + 1) * group_len)
                dscore = (prob * (dprob - delta)).astype(jnp.bfloat16)
                k_part = dot(dscore, q_block)
                v_part = dot(prob.astype(jnp.bfloat16), c_block)
                if index < group_at:
                    k_part = k_part + acc[0, rows, :]
                    v_part = v_part + acc[1, rows, :]
                if group_at == min(index + PAST, groups - 1):
                    k_low = (k_part * factor).astype(jnp.bfloat16)
                    grads[1, head, rows, :] = k_low
                    grads[2, head, rows, :] = v_part.astype(jnp.bfloat16)
                    k_terms = k_terms + jnp.sum(
                        k_low.astype(jnp.float32) * block(1, index).astype(jnp.float32),
                        axis=0,
                        keepdims=True,
                    )
                else:
                    acc[0, rows, :] = k_part
                    acc[1, rows, :] = v_part
                q_turned = q_turned + dot(turned[index], dscore)
            q_low = (jnp.transpose(q_turned) * factor).astype(jnp.bfloat16)
            grads[0, head, group_at * group_len : (group_at + 1) * group_len, :] = q_low
            q_terms = q_terms + jnp.sum(
                q_low.astype(jnp.float32) * q_block.astype(jnp.float32), axis=0, keepdims=True
            )
        terms[head, 0:1, :] = q_terms / q_gain[:, columns(me, head)]
        terms[head, 1:2, :] = k_terms / k_gain[:, columns(me, head)]
        for which, landing in ((0, back.at[0]), (1, back.at[1]), (2, v_out)):
            for step in range(1, owners):
                other, place = partner(step)
                pltpu.make_async_remote_copy(
                    src_ref=grads.at[which, head, pl.ds(pl.multiple_of(other * tokens, tokens), tokens)],
                    dst_ref=landing.at[:, columns(me, head)],
                    send_sem=back_send.at[which],
                    recv_sem=back_recv.at[which],
                    device_id=place,
                    device_id_type=MESH,
                ).start()
            pltpu.make_async_copy(
                grads.at[which, head, my_rows], landing.at[:, columns(me, head)], back_recv.at[which]
            ).start()
        return carry

    lax.fori_loop(0, per_owner, one_head, 0)

    target_rep = me // per_rep
    slot = rep * per_rep + lax.rem(me, per_rep)

    def send_terms(place):
        pltpu.make_async_remote_copy(
            src_ref=terms,
            dst_ref=gathered.at[slot],
            send_sem=terms_send,
            recv_sem=terms_recv,
            device_id={**place, "rep": target_rep},
            device_id_type=MESH,
        ).start()

    for step in range(1, owners):
        send_terms(partner(step)[1])

    @pl.when(rep != target_rep)
    def _():
        send_terms(partner(0)[1])

    @pl.when(rep == target_rep)
    def _():
        pltpu.make_async_copy(terms, gathered.at[slot], terms_recv).start()

    def denormalize_rows(which, gain_ref, out_ref):
        def step(index, carry):
            rows = pl.ds(pl.multiple_of(index * ROWS, ROWS), ROWS)
            values = raw[which, rows, :].astype(jnp.float32)
            scale = inv[which, rows, :]
            weighted = back[which, rows, :].astype(jnp.float32) * gain_ref[...]
            inner = jnp.mean(values * weighted, axis=-1, keepdims=True)
            result = scale * weighted - values * (scale * scale * scale * inner)
            out_ref[rows, :] = result.astype(jnp.bfloat16)
            return carry

        lax.fori_loop(0, tokens // ROWS, step, 0)

    for which, gain_ref, out_ref in ((0, q_gain, q_out), (1, k_gain, k_out)):
        pltpu.make_async_copy(back.at[which], back.at[which], back_recv.at[which]).wait()
        denormalize_rows(which, gain_ref, out_ref)

    pltpu.make_async_copy(gathered, gathered, terms_recv).wait()
    for sub in range(per_rep):
        for head in range(per_owner):
            lanes = slice((sub * per_owner + head) * HEAD_DIM, (sub * per_owner + head + 1) * HEAD_DIM)
            sums = sum(gathered[clip * per_rep + sub, head] for clip in range(reps))
            q_gain_out[lanes] = sums[0]
            k_gain_out[lanes] = sums[1]
    pltpu.make_async_copy(v_out, v_out, back_recv.at[2]).wait()

    pltpu.make_async_copy(few, few, first_send).wait()
    for which in range(4):
        for head in range(per_owner):
            sent = heads.at[which, head, pl.ds(0, (owners - 1) * tokens)]
            pltpu.make_async_copy(sent, sent, send_sem.at[which, head]).wait()
    for which in range(3):
        sent = grads.at[which, :, pl.ds(0, (owners - 1) * tokens)]
        pltpu.make_async_copy(sent, sent, back_send.at[which]).wait()
    sent = gathered.at[pl.ds(0, owners - 1)]
    pltpu.make_async_copy(sent, sent, terms_send).wait()

    @pl.when(rep != target_rep)
    def _():
        pltpu.make_async_copy(terms, terms, terms_send).wait()


def store_kernel(*refs):
    sources, targets, sems = refs[:5], refs[5:10], refs[10]
    copies = []
    for which, (source, target) in enumerate(zip(sources, targets)):
        parts = STORE_PARTS if len(source.shape) == 2 else 1
        step = source.shape[0] // parts
        for part in range(parts):
            piece = pl.ds(part * step, step)
            copies.append(
                pltpu.make_async_copy(source.at[piece], target.at[piece], sems.at[which, part])
            )
    for copy in copies:
        copy.start()
    for copy in copies:
        copy.wait()


def head_body(query_raw, key_raw, value_in, out_cotangent, query_gain, key_gain, attend_from):
    groups, seqs, reps = (lax.axis_size(name) for name in ("group", "seq", "rep"))
    tokens, width = query_raw.shape[2:]
    owners = groups * seqs
    per_owner = width // HEAD_DIM // owners
    group_len = seqs * tokens
    clip_len = owners * tokens
    low = jnp.bfloat16
    rows = jax.ShapeDtypeStruct((tokens, width), low)
    gain_rows = jax.ShapeDtypeStruct((width // reps,), jnp.float32)
    vmem = pl.BlockSpec(memory_space=pltpu.VMEM)
    hbm = pl.BlockSpec(memory_space=pltpu.HBM)
    anywhere = pl.BlockSpec(memory_space=pl.ANY)
    dma = pltpu.SemaphoreType.DMA
    sizes = (groups, seqs, reps, tokens, width, per_owner)
    results = pl.pallas_call(
        functools.partial(head_kernel, sizes),
        out_shape=(rows, rows, rows, gain_rows, gain_rows),
        in_specs=[pl.BlockSpec(memory_space=pltpu.SMEM)] + [hbm] * 4 + [vmem] * 2,
        out_specs=(vmem,) * 5,
        scratch_shapes=[
            pltpu.VMEM((2, tokens, width), low),
            pltpu.VMEM((2, tokens, width), low),
            pltpu.VMEM((2, tokens, 1), jnp.float32),
            pltpu.VMEM((4, per_owner, clip_len, HEAD_DIM), low),
            pltpu.VMEM((3, per_owner, clip_len, HEAD_DIM), low),
            pltpu.VMEM((2, tokens, width), low),
            pltpu.VMEM((owners, 8, group_len), jnp.float32),
            pltpu.VMEM((2, clip_len, HEAD_DIM), jnp.float32),
            pltpu.VMEM((per_owner, 8, HEAD_DIM), jnp.float32),
            pltpu.VMEM((owners, per_owner, 8, HEAD_DIM), jnp.float32),
            dma((2,)),
            dma((4, per_owner)),
            dma((4, per_owner)),
            dma((3,)),
            dma((3,)),
            dma,
            dma,
            dma,
            dma,
        ],
        compiler_params=pltpu.CompilerParams(
            collective_id=0, has_side_effects=True, vmem_limit_bytes=57 * 1024 * 1024
        ),
    )(
        attend_from,
        query_raw.reshape(tokens, width),
        key_raw.reshape(tokens, width),
        value_in.reshape(tokens, width),
        out_cotangent.reshape(tokens, width),
        query_gain.reshape(1, width),
        key_gain.reshape(1, width),
    )
    q_grad, k_grad, v_grad, q_gain_grad, k_gain_grad = pl.pallas_call(
        store_kernel,
        out_shape=(rows, rows, rows, gain_rows, gain_rows),
        in_specs=[vmem] * 5,
        out_specs=(anywhere,) * 5,
        scratch_shapes=[dma((5, STORE_PARTS))],
    )(*results)
    return (
        q_grad.reshape(query_raw.shape),
        k_grad.reshape(key_raw.shape),
        v_grad.reshape(value_in.shape),
        q_gain_grad,
        k_gain_grad,
    )


def ring_body(query_raw, key_raw, value_in, out_cotangent, query_gain, key_gain, attend_from):
    tok_rows = query_raw.shape[2]
    feature_width = query_raw.shape[3]
    q_values, q_inv, q_normed = normalize(query_raw.reshape(tok_rows, feature_width), query_gain)
    k_values, k_inv, k_normed = normalize(key_raw.reshape(tok_rows, feature_width), key_gain)
    heads_q, heads_k, heads_v, heads_cot = (
        lax.all_to_all(q_normed, "seq", split_axis=1, concat_axis=0, tiled=True),
        lax.all_to_all(k_normed, "seq", split_axis=1, concat_axis=0, tiled=True),
        lax.all_to_all(
            value_in.reshape(tok_rows, feature_width),
            "seq",
            split_axis=1,
            concat_axis=0,
            tiled=True,
        ),
        lax.all_to_all(
            out_cotangent.reshape(tok_rows, feature_width),
            "seq",
            split_axis=1,
            concat_axis=0,
            tiled=True,
        ),
    )
    group_len = heads_q.shape[0]
    head_width = heads_q.shape[1]
    window_len = PAST + 1
    own_pair = jnp.stack((heads_k, heads_v))
    earlier = []
    current = own_pair
    for hop_count in range(PAST):
        current = pass_forward(current, 1)
        earlier.insert(0, current)
    stacked = jnp.concatenate(earlier + [own_pair], axis=1)
    key_window = stacked[0]
    value_window = stacked[1]
    group_index = lax.axis_index("group")
    key_owner = (
        group_index - PAST + jnp.arange(window_len * group_len, dtype=jnp.int32) // group_len
    )
    visible = key_owner >= attend_from[0, 0]
    factor = HEAD_DIM ** (-0.5)
    query_block = 512 if group_len % 512 == 0 else group_len
    count_heads = head_width // HEAD_DIM
    key_rows_count = window_len * group_len

    def one_head(head_index, state_tuple):
        query_acc, key_acc, value_acc, max_acc, total_acc, delta_acc = state_tuple
        column_start = head_index * HEAD_DIM
        q_head = lax.dynamic_slice_in_dim(heads_q, column_start, HEAD_DIM, 1)
        cot_head = lax.dynamic_slice_in_dim(heads_cot, column_start, HEAD_DIM, 1)
        key_head = lax.dynamic_slice_in_dim(key_window, column_start, HEAD_DIM, 1)
        value_head = lax.dynamic_slice_in_dim(value_window, column_start, HEAD_DIM, 1)
        key_sum = jnp.zeros((key_rows_count, HEAD_DIM), jnp.float32)
        value_sum = jnp.zeros((key_rows_count, HEAD_DIM), jnp.float32)
        query_rows = []
        max_rows = []
        total_rows = []
        delta_rows = []
        for row_start in range(0, group_len, query_block):
            query_part, key_part, value_part, row_max, row_total, row_delta = head_pass(
                q_head[row_start : row_start + query_block],
                key_head,
                value_head,
                cot_head[row_start : row_start + query_block],
                visible,
                factor,
            )
            query_rows.append(query_part)
            max_rows.append(row_max)
            total_rows.append(row_total)
            delta_rows.append(row_delta)
            key_sum = key_sum + key_part
            value_sum = value_sum + value_part
        query_acc = lax.dynamic_update_slice_in_dim(
            query_acc, jnp.concatenate(query_rows, axis=0), column_start, 1
        )
        key_acc = lax.dynamic_update_slice_in_dim(key_acc, key_sum, column_start, 1)
        value_acc = lax.dynamic_update_slice_in_dim(value_acc, value_sum, column_start, 1)
        max_acc = lax.dynamic_update_slice_in_dim(
            max_acc, jnp.concatenate(max_rows)[:, None], head_index, 1
        )
        total_acc = lax.dynamic_update_slice_in_dim(
            total_acc, jnp.concatenate(total_rows)[:, None], head_index, 1
        )
        delta_acc = lax.dynamic_update_slice_in_dim(
            delta_acc, jnp.concatenate(delta_rows)[:, None], head_index, 1
        )
        return (query_acc, key_acc, value_acc, max_acc, total_acc, delta_acc)

    initial = (
        jnp.zeros((group_len, head_width), jnp.float32),
        jnp.zeros((key_rows_count, head_width), jnp.float32),
        jnp.zeros((key_rows_count, head_width), jnp.float32),
        jnp.zeros((group_len, count_heads), jnp.float32),
        jnp.zeros((group_len, count_heads), jnp.float32),
        jnp.zeros((group_len, count_heads), jnp.float32),
    )
    query_acc, key_acc, value_acc, max_all, total_all, delta_all = lax.fori_loop(
        0, count_heads, one_head, initial
    )
    cotangent_pair = jnp.stack((key_acc, value_acc))
    own_total = cotangent_pair[:, 0:group_len]
    for hop_count in range(1, PAST + 1):
        lower_row = hop_count * group_len
        own_total = pass_back(own_total, -1) + cotangent_pair[:, lower_row : lower_row + group_len]
    query_heads = query_acc.astype(jnp.bfloat16)
    key_heads = own_total[0].astype(jnp.bfloat16)
    value_heads = own_total[1].astype(jnp.bfloat16)
    token_q, token_k, token_v = (
        lax.all_to_all(query_heads, "seq", split_axis=0, concat_axis=1, tiled=True),
        lax.all_to_all(key_heads, "seq", split_axis=0, concat_axis=1, tiled=True),
        lax.all_to_all(value_heads, "seq", split_axis=0, concat_axis=1, tiled=True),
    )
    query_grad, query_terms = denormalize(q_values, q_inv, query_gain, token_q)
    key_grad, key_terms = denormalize(k_values, k_inv, key_gain, token_k)
    query_total, key_total_gain = lax.psum((query_terms, key_terms), ("group", "seq", "rep"))
    rep_width = feature_width // lax.axis_size("rep")
    offset = lax.axis_index("rep") * rep_width
    return (
        query_grad.reshape(query_raw.shape),
        key_grad.reshape(key_raw.shape),
        token_v.reshape(value_in.shape),
        lax.dynamic_slice_in_dim(query_total, offset, rep_width),
        lax.dynamic_slice_in_dim(key_total_gain, offset, rep_width),
    )


def body(*arrays):
    tokens, width = arrays[0].shape[2:]
    owners = lax.axis_size("group") * lax.axis_size("seq")
    heads = width // HEAD_DIM
    even = heads % owners == 0 and owners % lax.axis_size("rep") == 0
    if even and tokens * owners * heads <= 32768 and tokens % 16 == 0:
        return head_body(*arrays)
    return ring_body(*arrays)


def solution(mesh):
    placed = (
        P("rep", "group", "seq", None),
        P("rep", "group", "seq", None),
        P("rep", "group", "seq", None),
        P("rep", "group", "seq", None),
        P(),
        P(),
        P("rep", "group"),
    )
    return jax.shard_map(
        body,
        mesh=mesh,
        in_specs=placed,
        out_specs=(
            P("rep", "group", "seq", None),
            P("rep", "group", "seq", None),
            P("rep", "group", "seq", None),
            P("rep"),
            P("rep"),
        ),
        check_vma=False,
    )
```

```python
import functools

import jax
import jax.numpy as jnp
from jax import lax
from jax.experimental import pallas as pl
from jax.experimental.pallas import tpu as pltpu
from jax.sharding import PartitionSpec as P

HEAD_DIM = 128
PAST = 2


EPSILON = 1e-06


def from_behind(block, axis, distance):
    devices = range(lax.axis_size(axis))
    route = [(i - distance, i) for i in devices if i - distance in devices]
    return lax.ppermute(block, axis, route)


def normalize(row_values, gain_vec):
    values = row_values.astype(jnp.float32)
    inv_rms = lax.rsqrt(jnp.mean(values * values, axis=-1, keepdims=True) + EPSILON)
    return (values, inv_rms, (values * inv_rms * gain_vec).astype(jnp.bfloat16))


def denormalize(values, inv_rms, gain_vec, grad_low):
    upstream = grad_low.astype(jnp.float32)
    weighted = upstream * gain_vec
    inner_mean = jnp.mean(values * weighted, axis=-1, keepdims=True)
    result = inv_rms * weighted - values * (inv_rms * inv_rms * inv_rms) * inner_mean
    gain_terms = jnp.sum(upstream * values * inv_rms, axis=0)
    return (result.astype(jnp.bfloat16), gain_terms)


def head_pass(query_head, key_head, value_head, cot_head, visible, factor):
    scores = jnp.dot(query_head, key_head.T, preferred_element_type=jnp.float32) * factor
    scores = jnp.where(visible[None, :], scores, -1e30)
    row_max = jnp.max(scores, axis=1, keepdims=True)
    weights = jnp.exp(scores - row_max)
    row_total = jnp.sum(weights, axis=1, keepdims=True)
    probabilities = weights / row_total
    probs_low = probabilities.astype(jnp.bfloat16)
    dprobs = jnp.dot(cot_head, value_head.T, preferred_element_type=jnp.float32)
    row_delta = jnp.sum(probabilities * dprobs, axis=1, keepdims=True)
    dscores = (probabilities * (dprobs - row_delta)).astype(jnp.bfloat16)
    query_part = jnp.dot(dscores, key_head, preferred_element_type=jnp.float32) * factor
    key_part = jnp.dot(dscores.T, query_head, preferred_element_type=jnp.float32) * factor
    value_part = jnp.dot(probs_low.T, cot_head, preferred_element_type=jnp.float32)
    return (query_part, key_part, value_part, row_max[:, 0], row_total[:, 0], row_delta[:, 0])


def pass_forward(kv_pair, hop_count):
    return from_behind(kv_pair, "group", hop_count)


def pass_back(cotangent_pair, hop_count):
    return from_behind(cotangent_pair, "group", hop_count)


MESH = pl.DeviceIdType.MESH
ROWS = 16
STORE_PARTS = 4
NT = (((1,), (1,)), ((), ()))


def dot(left, right, dims=(((1,), (0,)), ((), ()))):
    return lax.dot_general(left, right, dims, preferred_element_type=jnp.float32)


def head_kernel(
    sizes,
    attend_ref, q_hbm, k_hbm, v_hbm, c_hbm, q_gain, k_gain,
    q_out, k_out, v_out, q_gain_out, k_gain_out,
    raw, normed, inv, heads, grads, back, first, acc, gathered, summed, totals,
    raw_sem, send_sem, recv_sem, back_send, back_recv,
    first_send, first_recv, clip_send, clip_recv, totals_send, totals_recv,
):
    groups, seqs, reps, tokens, width, per_owner = sizes
    owners = groups * seqs
    group_len = seqs * tokens
    own_width = per_owner * HEAD_DIM
    per_rep = owners // reps
    group, seq, rep = lax.axis_index("group"), lax.axis_index("seq"), lax.axis_index("rep")
    me = group * seqs + seq
    factor = HEAD_DIM ** (-0.5)

    def partner(step):
        other = lax.rem(me + step, owners)
        return other, {"group": other // seqs, "seq": lax.rem(other, seqs)}

    def clip_partner(step):
        return {"rep": lax.rem(rep + step, reps)}

    places = [partner(step)[1] for step in range(1, owners)]
    places += [clip_partner(step) for step in range(1, reps)]
    barrier = pltpu.get_barrier_semaphore()
    for place in places:
        pl.semaphore_signal(barrier, inc=1, device_id=place, device_id_type=MESH)

    loads = []
    for which, source in enumerate((q_hbm, k_hbm)):
        load = pltpu.make_async_copy(source, raw.at[which], raw_sem.at[which])
        load.start()
        loads.append(load)

    my_rows = pl.ds(pl.multiple_of(me * tokens, tokens), tokens)

    def columns(owner, head):
        return pl.ds(pl.multiple_of(owner * own_width + head * HEAD_DIM, HEAD_DIM), HEAD_DIM)

    def send_heads(which, source, head):
        for step in range(1, owners):
            other, place = partner(step)
            pltpu.make_async_remote_copy(
                src_ref=source.at[:, columns(other, head)],
                dst_ref=heads.at[which, head, my_rows],
                send_sem=send_sem.at[which, head],
                recv_sem=recv_sem.at[which, head],
                device_id=place,
                device_id_type=MESH,
            ).start()
        pltpu.make_async_copy(
            source.at[:, columns(me, head)], heads.at[which, head, my_rows], recv_sem.at[which, head]
        ).start()

    def normalize_rows(which, gain_ref):
        def step(index, carry):
            rows = pl.ds(pl.multiple_of(index * ROWS, ROWS), ROWS)
            values = raw[which, rows, :].astype(jnp.float32)
            scale = lax.rsqrt(jnp.mean(values * values, axis=-1, keepdims=True) + EPSILON)
            inv[which, rows, :] = scale
            normed[which, rows, :] = (values * scale * gain_ref[...]).astype(jnp.bfloat16)
            return carry

        lax.fori_loop(0, tokens // ROWS, step, 0)

    first[me] = jnp.full(first.shape[1:], attend_ref[0, 0].astype(jnp.float32))
    pl.semaphore_wait(barrier, len(places))
    for step in range(1, owners):
        other, place = partner(step)
        pltpu.make_async_remote_copy(
            src_ref=first.at[me],
            dst_ref=first.at[me],
            send_sem=first_send,
            recv_sem=first_recv,
            device_id=place,
            device_id_type=MESH,
        ).start()
    send_heads(2, v_hbm, 0)
    send_heads(3, c_hbm, 0)
    loads[0].wait()
    normalize_rows(0, q_gain)
    send_heads(0, normed.at[0], 0)
    loads[1].wait()
    normalize_rows(1, k_gain)
    send_heads(1, normed.at[1], 0)

    def send_rest(head, carry):
        for which, source in ((0, normed.at[0]), (1, normed.at[1]), (2, v_hbm), (3, c_hbm)):
            send_heads(which, source, head)
        return carry

    lax.fori_loop(1, per_owner, send_rest, 0)

    gathered[rep] = jnp.zeros(gathered.shape[1:], jnp.float32)
    few = first.at[pl.ds(0, owners - 1)]
    pltpu.make_async_copy(few, few, first_recv).wait()

    def one_head(head, carry):
        for which in range(4):
            whole = heads.at[which, head]
            pltpu.make_async_copy(whole, whole, recv_sem.at[which, head]).wait()

        def block(which, index):
            return heads[which, head, index * group_len : (index + 1) * group_len, :]

        turned = [jnp.transpose(block(1, index)) for index in range(groups)]
        q_terms = jnp.zeros((1, HEAD_DIM), jnp.float32)
        k_terms = jnp.zeros((1, HEAD_DIM), jnp.float32)
        for group_at in range(groups):
            low = max(0, group_at - PAST)
            window = range(low, group_at + 1)
            q_block, c_block = block(0, group_at), block(3, group_at)
            first_row = first[group_at * seqs, 0:1, :]
            scores = []
            for index in window:
                score = dot(block(1, index), q_block, NT) * factor
                if index < group_at:
                    score = score + jnp.where(first_row > index, -1e30, 0.0)
                scores.append(score)
            top = functools.reduce(
                jnp.maximum, [jnp.max(score, axis=0, keepdims=True) for score in scores]
            )
            weights = [jnp.exp(score - top) for score in scores]
            total = sum(jnp.sum(weight, axis=0, keepdims=True) for weight in weights)
            share = 1.0 / total
            probs = [weight * share for weight in weights]
            dprobs = [dot(block(2, index), c_block, NT) for index in window]
            delta = sum(
                jnp.sum(prob * dprob, axis=0, keepdims=True) for prob, dprob in zip(probs, dprobs)
            )
            q_turned = jnp.zeros((HEAD_DIM, group_len), jnp.float32)
            for index, prob, dprob in zip(window, probs, dprobs):
                rows = slice(index * group_len, (index + 1) * group_len)
                dscore = (prob * (dprob - delta)).astype(jnp.bfloat16)
                k_part = dot(dscore, q_block)
                v_part = dot(prob.astype(jnp.bfloat16), c_block)
                if index < group_at:
                    k_part = k_part + acc[0, rows, :]
                    v_part = v_part + acc[1, rows, :]
                if group_at == min(index + PAST, groups - 1):
                    k_low = (k_part * factor).astype(jnp.bfloat16)
                    grads[1, head, rows, :] = k_low
                    grads[2, head, rows, :] = v_part.astype(jnp.bfloat16)
                    k_terms = k_terms + jnp.sum(
                        k_low.astype(jnp.float32) * block(1, index).astype(jnp.float32),
                        axis=0,
                        keepdims=True,
                    )
                else:
                    acc[0, rows, :] = k_part
                    acc[1, rows, :] = v_part
                q_turned = q_turned + dot(turned[index], dscore)
            q_low = (jnp.transpose(q_turned) * factor).astype(jnp.bfloat16)
            grads[0, head, group_at * group_len : (group_at + 1) * group_len, :] = q_low
            q_terms = q_terms + jnp.sum(
                q_low.astype(jnp.float32) * q_block.astype(jnp.float32), axis=0, keepdims=True
            )
        gathered[rep, head, 0:1, :] = q_terms / q_gain[:, columns(me, head)]
        gathered[rep, head, 1:2, :] = k_terms / k_gain[:, columns(me, head)]
        for which, landing in ((0, back.at[0]), (1, back.at[1]), (2, v_out)):
            for step in range(1, owners):
                other, place = partner(step)
                pltpu.make_async_remote_copy(
                    src_ref=grads.at[which, head, pl.ds(pl.multiple_of(other * tokens, tokens), tokens)],
                    dst_ref=landing.at[:, columns(me, head)],
                    send_sem=back_send.at[which],
                    recv_sem=back_recv.at[which],
                    device_id=place,
                    device_id_type=MESH,
                ).start()
            pltpu.make_async_copy(
                grads.at[which, head, my_rows], landing.at[:, columns(me, head)], back_recv.at[which]
            ).start()
        return carry

    lax.fori_loop(0, per_owner, one_head, 0)

    for step in range(1, reps):
        pltpu.make_async_remote_copy(
            src_ref=gathered.at[rep],
            dst_ref=gathered.at[rep],
            send_sem=clip_send,
            recv_sem=clip_recv,
            device_id=clip_partner(step),
            device_id_type=MESH,
        ).start()

    def denormalize_rows(which, gain_ref, out_ref):
        def step(index, carry):
            rows = pl.ds(pl.multiple_of(index * ROWS, ROWS), ROWS)
            values = raw[which, rows, :].astype(jnp.float32)
            scale = inv[which, rows, :]
            weighted = back[which, rows, :].astype(jnp.float32) * gain_ref[...]
            inner = jnp.mean(values * weighted, axis=-1, keepdims=True)
            result = scale * weighted - values * (scale * scale * scale * inner)
            out_ref[rows, :] = result.astype(jnp.bfloat16)
            return carry

        lax.fori_loop(0, tokens // ROWS, step, 0)

    pltpu.make_async_copy(back.at[0], back.at[0], back_recv.at[0]).wait()
    denormalize_rows(0, q_gain, q_out)

    other_clips = gathered.at[pl.ds(0, reps - 1)]
    pltpu.make_async_copy(other_clips, other_clips, clip_recv).wait()
    summed[...] = sum(gathered[clip] for clip in range(reps))
    slot = lax.rem(me, per_rep)

    @pl.when(me // per_rep == rep)
    def _():
        for step in range(1, owners):
            pltpu.make_async_remote_copy(
                src_ref=summed,
                dst_ref=totals.at[slot],
                send_sem=totals_send,
                recv_sem=totals_recv,
                device_id=partner(step)[1],
                device_id_type=MESH,
            ).start()
        pltpu.make_async_copy(summed, totals.at[slot], totals_recv).start()

    pltpu.make_async_copy(back.at[1], back.at[1], back_recv.at[1]).wait()
    denormalize_rows(1, k_gain, k_out)

    pltpu.make_async_copy(totals, totals, totals_recv).wait()
    for sub in range(per_rep):
        for head in range(per_owner):
            lanes = slice((sub * per_owner + head) * HEAD_DIM, (sub * per_owner + head + 1) * HEAD_DIM)
            q_gain_out[lanes] = totals[sub, head, 0]
            k_gain_out[lanes] = totals[sub, head, 1]
    pltpu.make_async_copy(v_out, v_out, back_recv.at[2]).wait()

    pltpu.make_async_copy(few, few, first_send).wait()
    for which in range(4):
        for head in range(per_owner):
            sent = heads.at[which, head, pl.ds(0, (owners - 1) * tokens)]
            pltpu.make_async_copy(sent, sent, send_sem.at[which, head]).wait()
    for which in range(3):
        sent = grads.at[which, :, pl.ds(0, (owners - 1) * tokens)]
        pltpu.make_async_copy(sent, sent, back_send.at[which]).wait()
    pltpu.make_async_copy(other_clips, other_clips, clip_send).wait()

    @pl.when(me // per_rep == rep)
    def _():
        sent = acc.at[0, pl.ds(0, (owners - 1) * per_owner * 8)]
        pltpu.make_async_copy(sent, sent, totals_send).wait()


def store_kernel(*refs):
    sources, targets, sems = refs[:5], refs[5:10], refs[10]
    copies = []
    for which, (source, target) in enumerate(zip(sources, targets)):
        parts = STORE_PARTS if len(source.shape) == 2 else 1
        step = source.shape[0] // parts
        for part in range(parts):
            piece = pl.ds(part * step, step)
            copies.append(
                pltpu.make_async_copy(source.at[piece], target.at[piece], sems.at[which, part])
            )
    for copy in copies:
        copy.start()
    for copy in copies:
        copy.wait()


def head_body(query_raw, key_raw, value_in, out_cotangent, query_gain, key_gain, attend_from):
    groups, seqs, reps = (lax.axis_size(name) for name in ("group", "seq", "rep"))
    tokens, width = query_raw.shape[2:]
    owners = groups * seqs
    per_owner = width // HEAD_DIM // owners
    group_len = seqs * tokens
    clip_len = owners * tokens
    low = jnp.bfloat16
    rows = jax.ShapeDtypeStruct((tokens, width), low)
    gain_rows = jax.ShapeDtypeStruct((width // reps,), jnp.float32)
    vmem = pl.BlockSpec(memory_space=pltpu.VMEM)
    hbm = pl.BlockSpec(memory_space=pltpu.HBM)
    anywhere = pl.BlockSpec(memory_space=pl.ANY)
    dma = pltpu.SemaphoreType.DMA
    sizes = (groups, seqs, reps, tokens, width, per_owner)
    results = pl.pallas_call(
        functools.partial(head_kernel, sizes),
        out_shape=(rows, rows, rows, gain_rows, gain_rows),
        in_specs=[pl.BlockSpec(memory_space=pltpu.SMEM)] + [hbm] * 4 + [vmem] * 2,
        out_specs=(vmem,) * 5,
        scratch_shapes=[
            pltpu.VMEM((2, tokens, width), low),
            pltpu.VMEM((2, tokens, width), low),
            pltpu.VMEM((2, tokens, 1), jnp.float32),
            pltpu.VMEM((4, per_owner, clip_len, HEAD_DIM), low),
            pltpu.VMEM((3, per_owner, clip_len, HEAD_DIM), low),
            pltpu.VMEM((2, tokens, width), low),
            pltpu.VMEM((owners, 8, group_len), jnp.float32),
            pltpu.VMEM((2, clip_len, HEAD_DIM), jnp.float32),
            pltpu.VMEM((reps, per_owner, 8, HEAD_DIM), jnp.float32),
            pltpu.VMEM((per_owner, 8, HEAD_DIM), jnp.float32),
            pltpu.VMEM((owners // reps, per_owner, 8, HEAD_DIM), jnp.float32),
            dma((2,)),
            dma((4, per_owner)),
            dma((4, per_owner)),
            dma((3,)),
            dma((3,)),
            dma,
            dma,
            dma,
            dma,
            dma,
            dma,
        ],
        compiler_params=pltpu.CompilerParams(
            collective_id=0, has_side_effects=True, vmem_limit_bytes=57 * 1024 * 1024
        ),
    )(
        attend_from,
        query_raw.reshape(tokens, width),
        key_raw.reshape(tokens, width),
        value_in.reshape(tokens, width),
        out_cotangent.reshape(tokens, width),
        query_gain.reshape(1, width),
        key_gain.reshape(1, width),
    )
    q_grad, k_grad, v_grad, q_gain_grad, k_gain_grad = pl.pallas_call(
        store_kernel,
        out_shape=(rows, rows, rows, gain_rows, gain_rows),
        in_specs=[vmem] * 5,
        out_specs=(anywhere,) * 5,
        scratch_shapes=[dma((5, STORE_PARTS))],
    )(*results)
    return (
        q_grad.reshape(query_raw.shape),
        k_grad.reshape(key_raw.shape),
        v_grad.reshape(value_in.shape),
        q_gain_grad,
        k_gain_grad,
    )


def ring_body(query_raw, key_raw, value_in, out_cotangent, query_gain, key_gain, attend_from):
    tok_rows = query_raw.shape[2]
    feature_width = query_raw.shape[3]
    q_values, q_inv, q_normed = normalize(query_raw.reshape(tok_rows, feature_width), query_gain)
    k_values, k_inv, k_normed = normalize(key_raw.reshape(tok_rows, feature_width), key_gain)
    heads_q, heads_k, heads_v, heads_cot = (
        lax.all_to_all(q_normed, "seq", split_axis=1, concat_axis=0, tiled=True),
        lax.all_to_all(k_normed, "seq", split_axis=1, concat_axis=0, tiled=True),
        lax.all_to_all(
            value_in.reshape(tok_rows, feature_width),
            "seq",
            split_axis=1,
            concat_axis=0,
            tiled=True,
        ),
        lax.all_to_all(
            out_cotangent.reshape(tok_rows, feature_width),
            "seq",
            split_axis=1,
            concat_axis=0,
            tiled=True,
        ),
    )
    group_len = heads_q.shape[0]
    head_width = heads_q.shape[1]
    window_len = PAST + 1
    own_pair = jnp.stack((heads_k, heads_v))
    earlier = []
    current = own_pair
    for hop_count in range(PAST):
        current = pass_forward(current, 1)
        earlier.insert(0, current)
    stacked = jnp.concatenate(earlier + [own_pair], axis=1)
    key_window = stacked[0]
    value_window = stacked[1]
    group_index = lax.axis_index("group")
    key_owner = (
        group_index - PAST + jnp.arange(window_len * group_len, dtype=jnp.int32) // group_len
    )
    visible = key_owner >= attend_from[0, 0]
    factor = HEAD_DIM ** (-0.5)
    query_block = 512 if group_len % 512 == 0 else group_len
    count_heads = head_width // HEAD_DIM
    key_rows_count = window_len * group_len

    def one_head(head_index, state_tuple):
        query_acc, key_acc, value_acc, max_acc, total_acc, delta_acc = state_tuple
        column_start = head_index * HEAD_DIM
        q_head = lax.dynamic_slice_in_dim(heads_q, column_start, HEAD_DIM, 1)
        cot_head = lax.dynamic_slice_in_dim(heads_cot, column_start, HEAD_DIM, 1)
        key_head = lax.dynamic_slice_in_dim(key_window, column_start, HEAD_DIM, 1)
        value_head = lax.dynamic_slice_in_dim(value_window, column_start, HEAD_DIM, 1)
        key_sum = jnp.zeros((key_rows_count, HEAD_DIM), jnp.float32)
        value_sum = jnp.zeros((key_rows_count, HEAD_DIM), jnp.float32)
        query_rows = []
        max_rows = []
        total_rows = []
        delta_rows = []
        for row_start in range(0, group_len, query_block):
            query_part, key_part, value_part, row_max, row_total, row_delta = head_pass(
                q_head[row_start : row_start + query_block],
                key_head,
                value_head,
                cot_head[row_start : row_start + query_block],
                visible,
                factor,
            )
            query_rows.append(query_part)
            max_rows.append(row_max)
            total_rows.append(row_total)
            delta_rows.append(row_delta)
            key_sum = key_sum + key_part
            value_sum = value_sum + value_part
        query_acc = lax.dynamic_update_slice_in_dim(
            query_acc, jnp.concatenate(query_rows, axis=0), column_start, 1
        )
        key_acc = lax.dynamic_update_slice_in_dim(key_acc, key_sum, column_start, 1)
        value_acc = lax.dynamic_update_slice_in_dim(value_acc, value_sum, column_start, 1)
        max_acc = lax.dynamic_update_slice_in_dim(
            max_acc, jnp.concatenate(max_rows)[:, None], head_index, 1
        )
        total_acc = lax.dynamic_update_slice_in_dim(
            total_acc, jnp.concatenate(total_rows)[:, None], head_index, 1
        )
        delta_acc = lax.dynamic_update_slice_in_dim(
            delta_acc, jnp.concatenate(delta_rows)[:, None], head_index, 1
        )
        return (query_acc, key_acc, value_acc, max_acc, total_acc, delta_acc)

    initial = (
        jnp.zeros((group_len, head_width), jnp.float32),
        jnp.zeros((key_rows_count, head_width), jnp.float32),
        jnp.zeros((key_rows_count, head_width), jnp.float32),
        jnp.zeros((group_len, count_heads), jnp.float32),
        jnp.zeros((group_len, count_heads), jnp.float32),
        jnp.zeros((group_len, count_heads), jnp.float32),
    )
    query_acc, key_acc, value_acc, max_all, total_all, delta_all = lax.fori_loop(
        0, count_heads, one_head, initial
    )
    cotangent_pair = jnp.stack((key_acc, value_acc))
    own_total = cotangent_pair[:, 0:group_len]
    for hop_count in range(1, PAST + 1):
        lower_row = hop_count * group_len
        own_total = pass_back(own_total, -1) + cotangent_pair[:, lower_row : lower_row + group_len]
    query_heads = query_acc.astype(jnp.bfloat16)
    key_heads = own_total[0].astype(jnp.bfloat16)
    value_heads = own_total[1].astype(jnp.bfloat16)
    token_q, token_k, token_v = (
        lax.all_to_all(query_heads, "seq", split_axis=0, concat_axis=1, tiled=True),
        lax.all_to_all(key_heads, "seq", split_axis=0, concat_axis=1, tiled=True),
        lax.all_to_all(value_heads, "seq", split_axis=0, concat_axis=1, tiled=True),
    )
    query_grad, query_terms = denormalize(q_values, q_inv, query_gain, token_q)
    key_grad, key_terms = denormalize(k_values, k_inv, key_gain, token_k)
    query_total, key_total_gain = lax.psum((query_terms, key_terms), ("group", "seq", "rep"))
    rep_width = feature_width // lax.axis_size("rep")
    offset = lax.axis_index("rep") * rep_width
    return (
        query_grad.reshape(query_raw.shape),
        key_grad.reshape(key_raw.shape),
        token_v.reshape(value_in.shape),
        lax.dynamic_slice_in_dim(query_total, offset, rep_width),
        lax.dynamic_slice_in_dim(key_total_gain, offset, rep_width),
    )


def body(*arrays):
    tokens, width = arrays[0].shape[2:]
    owners = lax.axis_size("group") * lax.axis_size("seq")
    heads = width // HEAD_DIM
    even = heads % owners == 0 and owners % lax.axis_size("rep") == 0
    if even and tokens * owners * heads <= 32768 and tokens % 16 == 0 and tokens * owners >= heads * 8:
        return head_body(*arrays)
    return ring_body(*arrays)


def solution(mesh):
    placed = (
        P("rep", "group", "seq", None),
        P("rep", "group", "seq", None),
        P("rep", "group", "seq", None),
        P("rep", "group", "seq", None),
        P(),
        P(),
        P("rep", "group"),
    )
    return jax.shard_map(
        body,
        mesh=mesh,
        in_specs=placed,
        out_specs=(
            P("rep", "group", "seq", None),
            P("rep", "group", "seq", None),
            P("rep", "group", "seq", None),
            P("rep"),
            P("rep"),
        ),
        check_vma=False,
    )
```

```python
import functools

import jax
import jax.numpy as jnp
from jax import lax
from jax.experimental import pallas as pl
from jax.experimental.pallas import tpu as pltpu
from jax.sharding import PartitionSpec as P

HEAD_DIM = 128
PAST = 2


EPSILON = 1e-06


def from_behind(block, axis, distance):
    devices = range(lax.axis_size(axis))
    route = [(i - distance, i) for i in devices if i - distance in devices]
    return lax.ppermute(block, axis, route)


def normalize(row_values, gain_vec):
    values = row_values.astype(jnp.float32)
    inv_rms = lax.rsqrt(jnp.mean(values * values, axis=-1, keepdims=True) + EPSILON)
    return (values, inv_rms, (values * inv_rms * gain_vec).astype(jnp.bfloat16))


def denormalize(values, inv_rms, gain_vec, grad_low):
    upstream = grad_low.astype(jnp.float32)
    weighted = upstream * gain_vec
    inner_mean = jnp.mean(values * weighted, axis=-1, keepdims=True)
    result = inv_rms * weighted - values * (inv_rms * inv_rms * inv_rms) * inner_mean
    gain_terms = jnp.sum(upstream * values * inv_rms, axis=0)
    return (result.astype(jnp.bfloat16), gain_terms)


def head_pass(query_head, key_head, value_head, cot_head, visible, factor):
    scores = jnp.dot(query_head, key_head.T, preferred_element_type=jnp.float32) * factor
    scores = jnp.where(visible[None, :], scores, -1e30)
    row_max = jnp.max(scores, axis=1, keepdims=True)
    weights = jnp.exp(scores - row_max)
    row_total = jnp.sum(weights, axis=1, keepdims=True)
    probabilities = weights / row_total
    probs_low = probabilities.astype(jnp.bfloat16)
    dprobs = jnp.dot(cot_head, value_head.T, preferred_element_type=jnp.float32)
    row_delta = jnp.sum(probabilities * dprobs, axis=1, keepdims=True)
    dscores = (probabilities * (dprobs - row_delta)).astype(jnp.bfloat16)
    query_part = jnp.dot(dscores, key_head, preferred_element_type=jnp.float32) * factor
    key_part = jnp.dot(dscores.T, query_head, preferred_element_type=jnp.float32) * factor
    value_part = jnp.dot(probs_low.T, cot_head, preferred_element_type=jnp.float32)
    return (query_part, key_part, value_part, row_max[:, 0], row_total[:, 0], row_delta[:, 0])


def pass_forward(kv_pair, hop_count):
    return from_behind(kv_pair, "group", hop_count)


def pass_back(cotangent_pair, hop_count):
    return from_behind(cotangent_pair, "group", hop_count)


MESH = pl.DeviceIdType.MESH
ROWS = 16
STORE_PARTS = 4
NT = (((1,), (1,)), ((), ()))


def dot(left, right, dims=(((1,), (0,)), ((), ()))):
    return lax.dot_general(left, right, dims, preferred_element_type=jnp.float32)


def head_kernel(
    sizes,
    attend_ref, q_hbm, k_hbm, v_hbm, c_hbm, q_gain, k_gain,
    q_out, k_out, v_out, q_gain_out, k_gain_out,
    raw, normed, inv, heads, grads, back, first, acc, gathered, summed, totals,
    raw_sem, send_sem, recv_sem, back_send, back_recv,
    first_send, first_recv, clip_send, clip_recv, totals_send, totals_recv,
):
    groups, seqs, reps, tokens, width, per_owner = sizes
    owners = groups * seqs
    group_len = seqs * tokens
    own_width = per_owner * HEAD_DIM
    per_rep = owners // reps
    group, seq, rep = lax.axis_index("group"), lax.axis_index("seq"), lax.axis_index("rep")
    me = group * seqs + seq
    order = sorted(range(1, owners), key=lambda step: step == seqs)
    factor = HEAD_DIM ** (-0.5)

    def partner(step):
        other = jnp.bitwise_xor(me, step)
        return other, {"group": other // seqs, "seq": lax.rem(other, seqs)}

    def clip_partner(step):
        return {"rep": lax.rem(rep + step, reps)}

    places = [partner(step)[1] for step in order]
    places += [clip_partner(step) for step in range(1, reps)]
    barrier = pltpu.get_barrier_semaphore()
    for place in places:
        pl.semaphore_signal(barrier, inc=1, device_id=place, device_id_type=MESH)

    loads = []
    for which, source in enumerate((q_hbm, k_hbm)):
        load = pltpu.make_async_copy(source, raw.at[which], raw_sem.at[which])
        load.start()
        loads.append(load)

    my_rows = pl.ds(pl.multiple_of(me * tokens, tokens), tokens)

    def columns(owner, head):
        return pl.ds(pl.multiple_of(owner * own_width + head * HEAD_DIM, HEAD_DIM), HEAD_DIM)

    def send_heads(which, source, head):
        for step in order:
            other, place = partner(step)
            pltpu.make_async_remote_copy(
                src_ref=source.at[:, columns(other, head)],
                dst_ref=heads.at[which, head, my_rows],
                send_sem=send_sem.at[which, head],
                recv_sem=recv_sem.at[which, head],
                device_id=place,
                device_id_type=MESH,
            ).start()
        pltpu.make_async_copy(
            source.at[:, columns(me, head)], heads.at[which, head, my_rows], recv_sem.at[which, head]
        ).start()

    def normalize_rows(which, gain_ref):
        def step(index, carry):
            rows = pl.ds(pl.multiple_of(index * ROWS, ROWS), ROWS)
            values = raw[which, rows, :].astype(jnp.float32)
            scale = lax.rsqrt(jnp.mean(values * values, axis=-1, keepdims=True) + EPSILON)
            inv[which, rows, :] = scale
            normed[which, rows, :] = (values * scale * gain_ref[...]).astype(jnp.bfloat16)
            return carry

        lax.fori_loop(0, tokens // ROWS, step, 0)

    first[me] = jnp.full(first.shape[1:], attend_ref[0, 0].astype(jnp.float32))
    pl.semaphore_wait(barrier, len(places))
    for step in order:
        other, place = partner(step)
        pltpu.make_async_remote_copy(
            src_ref=first.at[me],
            dst_ref=first.at[me],
            send_sem=first_send,
            recv_sem=first_recv,
            device_id=place,
            device_id_type=MESH,
        ).start()
    send_heads(2, v_hbm, 0)
    send_heads(3, c_hbm, 0)
    loads[0].wait()
    normalize_rows(0, q_gain)
    send_heads(0, normed.at[0], 0)
    loads[1].wait()
    normalize_rows(1, k_gain)
    send_heads(1, normed.at[1], 0)

    def send_rest(head, carry):
        for which, source in ((0, normed.at[0]), (1, normed.at[1]), (2, v_hbm), (3, c_hbm)):
            send_heads(which, source, head)
        return carry

    lax.fori_loop(1, per_owner, send_rest, 0)

    gathered[rep] = jnp.zeros(gathered.shape[1:], jnp.float32)
    few = first.at[pl.ds(0, owners - 1)]
    pltpu.make_async_copy(few, few, first_recv).wait()

    def one_head(head, carry):
        for which in range(4):
            whole = heads.at[which, head]
            pltpu.make_async_copy(whole, whole, recv_sem.at[which, head]).wait()

        def block(which, index):
            return heads[which, head, index * group_len : (index + 1) * group_len, :]

        turned = [jnp.transpose(block(1, index)) for index in range(groups)]
        q_terms = jnp.zeros((1, HEAD_DIM), jnp.float32)
        k_terms = jnp.zeros((1, HEAD_DIM), jnp.float32)
        for group_at in range(groups):
            low = max(0, group_at - PAST)
            window = range(low, group_at + 1)
            q_block, c_block = block(0, group_at), block(3, group_at)
            first_row = first[group_at * seqs, 0:1, :]
            scores = []
            for index in window:
                score = dot(block(1, index), q_block, NT) * factor
                if index < group_at:
                    score = score + jnp.where(first_row > index, -1e30, 0.0)
                scores.append(score)
            top = functools.reduce(
                jnp.maximum, [jnp.max(score, axis=0, keepdims=True) for score in scores]
            )
            weights = [jnp.exp(score - top) for score in scores]
            total = sum(jnp.sum(weight, axis=0, keepdims=True) for weight in weights)
            share = 1.0 / total
            probs = [weight * share for weight in weights]
            dprobs = [dot(block(2, index), c_block, NT) for index in window]
            delta = sum(
                jnp.sum(prob * dprob, axis=0, keepdims=True) for prob, dprob in zip(probs, dprobs)
            )
            q_turned = jnp.zeros((HEAD_DIM, group_len), jnp.float32)
            for index, prob, dprob in zip(window, probs, dprobs):
                rows = slice(index * group_len, (index + 1) * group_len)
                dscore = (prob * (dprob - delta)).astype(jnp.bfloat16)
                k_part = dot(dscore, q_block)
                v_part = dot(prob.astype(jnp.bfloat16), c_block)
                if index < group_at:
                    k_part = k_part + acc[0, rows, :]
                    v_part = v_part + acc[1, rows, :]
                if group_at == min(index + PAST, groups - 1):
                    k_low = (k_part * factor).astype(jnp.bfloat16)
                    grads[1, head, rows, :] = k_low
                    grads[2, head, rows, :] = v_part.astype(jnp.bfloat16)
                    k_terms = k_terms + jnp.sum(
                        k_low.astype(jnp.float32) * block(1, index).astype(jnp.float32),
                        axis=0,
                        keepdims=True,
                    )
                else:
                    acc[0, rows, :] = k_part
                    acc[1, rows, :] = v_part
                q_turned = q_turned + dot(turned[index], dscore)
            q_low = (jnp.transpose(q_turned) * factor).astype(jnp.bfloat16)
            grads[0, head, group_at * group_len : (group_at + 1) * group_len, :] = q_low
            q_terms = q_terms + jnp.sum(
                q_low.astype(jnp.float32) * q_block.astype(jnp.float32), axis=0, keepdims=True
            )
        gathered[rep, head, 0:1, :] = q_terms / q_gain[:, columns(me, head)]
        gathered[rep, head, 1:2, :] = k_terms / k_gain[:, columns(me, head)]
        for which, landing in ((0, back.at[0]), (1, back.at[1]), (2, v_out)):
            for step in order:
                other, place = partner(step)
                pltpu.make_async_remote_copy(
                    src_ref=grads.at[which, head, pl.ds(pl.multiple_of(other * tokens, tokens), tokens)],
                    dst_ref=landing.at[:, columns(me, head)],
                    send_sem=back_send.at[which],
                    recv_sem=back_recv.at[which],
                    device_id=place,
                    device_id_type=MESH,
                ).start()
            pltpu.make_async_copy(
                grads.at[which, head, my_rows], landing.at[:, columns(me, head)], back_recv.at[which]
            ).start()
        return carry

    lax.fori_loop(0, per_owner, one_head, 0)

    for step in range(1, reps):
        pltpu.make_async_remote_copy(
            src_ref=gathered.at[rep],
            dst_ref=gathered.at[rep],
            send_sem=clip_send,
            recv_sem=clip_recv,
            device_id=clip_partner(step),
            device_id_type=MESH,
        ).start()

    def denormalize_rows(which, gain_ref, out_ref):
        def step(index, carry):
            rows = pl.ds(pl.multiple_of(index * ROWS, ROWS), ROWS)
            values = raw[which, rows, :].astype(jnp.float32)
            scale = inv[which, rows, :]
            weighted = back[which, rows, :].astype(jnp.float32) * gain_ref[...]
            inner = jnp.mean(values * weighted, axis=-1, keepdims=True)
            result = scale * weighted - values * (scale * scale * scale * inner)
            out_ref[rows, :] = result.astype(jnp.bfloat16)
            return carry

        lax.fori_loop(0, tokens // ROWS, step, 0)

    pltpu.make_async_copy(back.at[0], back.at[0], back_recv.at[0]).wait()
    denormalize_rows(0, q_gain, q_out)

    other_clips = gathered.at[pl.ds(0, reps - 1)]
    pltpu.make_async_copy(other_clips, other_clips, clip_recv).wait()
    summed[...] = sum(gathered[clip] for clip in range(reps))
    slot = lax.rem(me, per_rep)

    @pl.when(me // per_rep == rep)
    def _():
        for step in order:
            pltpu.make_async_remote_copy(
                src_ref=summed,
                dst_ref=totals.at[slot],
                send_sem=totals_send,
                recv_sem=totals_recv,
                device_id=partner(step)[1],
                device_id_type=MESH,
            ).start()
        pltpu.make_async_copy(summed, totals.at[slot], totals_recv).start()

    pltpu.make_async_copy(back.at[1], back.at[1], back_recv.at[1]).wait()
    denormalize_rows(1, k_gain, k_out)

    pltpu.make_async_copy(totals, totals, totals_recv).wait()
    for sub in range(per_rep):
        for head in range(per_owner):
            lanes = slice((sub * per_owner + head) * HEAD_DIM, (sub * per_owner + head + 1) * HEAD_DIM)
            q_gain_out[lanes] = totals[sub, head, 0]
            k_gain_out[lanes] = totals[sub, head, 1]
    pltpu.make_async_copy(v_out, v_out, back_recv.at[2]).wait()

    pltpu.make_async_copy(few, few, first_send).wait()
    for which in range(4):
        for head in range(per_owner):
            sent = heads.at[which, head, pl.ds(0, (owners - 1) * tokens)]
            pltpu.make_async_copy(sent, sent, send_sem.at[which, head]).wait()
    for which in range(3):
        sent = grads.at[which, :, pl.ds(0, (owners - 1) * tokens)]
        pltpu.make_async_copy(sent, sent, back_send.at[which]).wait()
    pltpu.make_async_copy(other_clips, other_clips, clip_send).wait()

    @pl.when(me // per_rep == rep)
    def _():
        sent = acc.at[0, pl.ds(0, (owners - 1) * per_owner * 8)]
        pltpu.make_async_copy(sent, sent, totals_send).wait()


def store_kernel(*refs):
    sources, targets, sems = refs[:5], refs[5:10], refs[10]
    copies = []
    for which, (source, target) in enumerate(zip(sources, targets)):
        parts = STORE_PARTS if len(source.shape) == 2 else 1
        step = source.shape[0] // parts
        for part in range(parts):
            piece = pl.ds(part * step, step)
            copies.append(
                pltpu.make_async_copy(source.at[piece], target.at[piece], sems.at[which, part])
            )
    for copy in copies:
        copy.start()
    for copy in copies:
        copy.wait()


def head_body(query_raw, key_raw, value_in, out_cotangent, query_gain, key_gain, attend_from):
    groups, seqs, reps = (lax.axis_size(name) for name in ("group", "seq", "rep"))
    tokens, width = query_raw.shape[2:]
    owners = groups * seqs
    per_owner = width // HEAD_DIM // owners
    group_len = seqs * tokens
    clip_len = owners * tokens
    low = jnp.bfloat16
    rows = jax.ShapeDtypeStruct((tokens, width), low)
    gain_rows = jax.ShapeDtypeStruct((width // reps,), jnp.float32)
    vmem = pl.BlockSpec(memory_space=pltpu.VMEM)
    hbm = pl.BlockSpec(memory_space=pltpu.HBM)
    anywhere = pl.BlockSpec(memory_space=pl.ANY)
    dma = pltpu.SemaphoreType.DMA
    sizes = (groups, seqs, reps, tokens, width, per_owner)
    results = pl.pallas_call(
        functools.partial(head_kernel, sizes),
        out_shape=(rows, rows, rows, gain_rows, gain_rows),
        in_specs=[pl.BlockSpec(memory_space=pltpu.SMEM)] + [hbm] * 4 + [vmem] * 2,
        out_specs=(vmem,) * 5,
        scratch_shapes=[
            pltpu.VMEM((2, tokens, width), low),
            pltpu.VMEM((2, tokens, width), low),
            pltpu.VMEM((2, tokens, 1), jnp.float32),
            pltpu.VMEM((4, per_owner, clip_len, HEAD_DIM), low),
            pltpu.VMEM((3, per_owner, clip_len, HEAD_DIM), low),
            pltpu.VMEM((2, tokens, width), low),
            pltpu.VMEM((owners, 8, group_len), jnp.float32),
            pltpu.VMEM((2, clip_len, HEAD_DIM), jnp.float32),
            pltpu.VMEM((reps, per_owner, 8, HEAD_DIM), jnp.float32),
            pltpu.VMEM((per_owner, 8, HEAD_DIM), jnp.float32),
            pltpu.VMEM((owners // reps, per_owner, 8, HEAD_DIM), jnp.float32),
            dma((2,)),
            dma((4, per_owner)),
            dma((4, per_owner)),
            dma((3,)),
            dma((3,)),
            dma,
            dma,
            dma,
            dma,
            dma,
            dma,
        ],
        compiler_params=pltpu.CompilerParams(
            collective_id=0, has_side_effects=True, vmem_limit_bytes=57 * 1024 * 1024
        ),
    )(
        attend_from,
        query_raw.reshape(tokens, width),
        key_raw.reshape(tokens, width),
        value_in.reshape(tokens, width),
        out_cotangent.reshape(tokens, width),
        query_gain.reshape(1, width),
        key_gain.reshape(1, width),
    )
    q_grad, k_grad, v_grad, q_gain_grad, k_gain_grad = pl.pallas_call(
        store_kernel,
        out_shape=(rows, rows, rows, gain_rows, gain_rows),
        in_specs=[vmem] * 5,
        out_specs=(anywhere,) * 5,
        scratch_shapes=[dma((5, STORE_PARTS))],
    )(*results)
    return (
        q_grad.reshape(query_raw.shape),
        k_grad.reshape(key_raw.shape),
        v_grad.reshape(value_in.shape),
        q_gain_grad,
        k_gain_grad,
    )


def ring_body(query_raw, key_raw, value_in, out_cotangent, query_gain, key_gain, attend_from):
    tok_rows = query_raw.shape[2]
    feature_width = query_raw.shape[3]
    q_values, q_inv, q_normed = normalize(query_raw.reshape(tok_rows, feature_width), query_gain)
    k_values, k_inv, k_normed = normalize(key_raw.reshape(tok_rows, feature_width), key_gain)
    heads_q, heads_k, heads_v, heads_cot = (
        lax.all_to_all(q_normed, "seq", split_axis=1, concat_axis=0, tiled=True),
        lax.all_to_all(k_normed, "seq", split_axis=1, concat_axis=0, tiled=True),
        lax.all_to_all(
            value_in.reshape(tok_rows, feature_width),
            "seq",
            split_axis=1,
            concat_axis=0,
            tiled=True,
        ),
        lax.all_to_all(
            out_cotangent.reshape(tok_rows, feature_width),
            "seq",
            split_axis=1,
            concat_axis=0,
            tiled=True,
        ),
    )
    group_len = heads_q.shape[0]
    head_width = heads_q.shape[1]
    window_len = PAST + 1
    own_pair = jnp.stack((heads_k, heads_v))
    earlier = []
    current = own_pair
    for hop_count in range(PAST):
        current = pass_forward(current, 1)
        earlier.insert(0, current)
    stacked = jnp.concatenate(earlier + [own_pair], axis=1)
    key_window = stacked[0]
    value_window = stacked[1]
    group_index = lax.axis_index("group")
    key_owner = (
        group_index - PAST + jnp.arange(window_len * group_len, dtype=jnp.int32) // group_len
    )
    visible = key_owner >= attend_from[0, 0]
    factor = HEAD_DIM ** (-0.5)
    query_block = 512 if group_len % 512 == 0 else group_len
    count_heads = head_width // HEAD_DIM
    key_rows_count = window_len * group_len

    def one_head(head_index, state_tuple):
        query_acc, key_acc, value_acc, max_acc, total_acc, delta_acc = state_tuple
        column_start = head_index * HEAD_DIM
        q_head = lax.dynamic_slice_in_dim(heads_q, column_start, HEAD_DIM, 1)
        cot_head = lax.dynamic_slice_in_dim(heads_cot, column_start, HEAD_DIM, 1)
        key_head = lax.dynamic_slice_in_dim(key_window, column_start, HEAD_DIM, 1)
        value_head = lax.dynamic_slice_in_dim(value_window, column_start, HEAD_DIM, 1)
        key_sum = jnp.zeros((key_rows_count, HEAD_DIM), jnp.float32)
        value_sum = jnp.zeros((key_rows_count, HEAD_DIM), jnp.float32)
        query_rows = []
        max_rows = []
        total_rows = []
        delta_rows = []
        for row_start in range(0, group_len, query_block):
            query_part, key_part, value_part, row_max, row_total, row_delta = head_pass(
                q_head[row_start : row_start + query_block],
                key_head,
                value_head,
                cot_head[row_start : row_start + query_block],
                visible,
                factor,
            )
            query_rows.append(query_part)
            max_rows.append(row_max)
            total_rows.append(row_total)
            delta_rows.append(row_delta)
            key_sum = key_sum + key_part
            value_sum = value_sum + value_part
        query_acc = lax.dynamic_update_slice_in_dim(
            query_acc, jnp.concatenate(query_rows, axis=0), column_start, 1
        )
        key_acc = lax.dynamic_update_slice_in_dim(key_acc, key_sum, column_start, 1)
        value_acc = lax.dynamic_update_slice_in_dim(value_acc, value_sum, column_start, 1)
        max_acc = lax.dynamic_update_slice_in_dim(
            max_acc, jnp.concatenate(max_rows)[:, None], head_index, 1
        )
        total_acc = lax.dynamic_update_slice_in_dim(
            total_acc, jnp.concatenate(total_rows)[:, None], head_index, 1
        )
        delta_acc = lax.dynamic_update_slice_in_dim(
            delta_acc, jnp.concatenate(delta_rows)[:, None], head_index, 1
        )
        return (query_acc, key_acc, value_acc, max_acc, total_acc, delta_acc)

    initial = (
        jnp.zeros((group_len, head_width), jnp.float32),
        jnp.zeros((key_rows_count, head_width), jnp.float32),
        jnp.zeros((key_rows_count, head_width), jnp.float32),
        jnp.zeros((group_len, count_heads), jnp.float32),
        jnp.zeros((group_len, count_heads), jnp.float32),
        jnp.zeros((group_len, count_heads), jnp.float32),
    )
    query_acc, key_acc, value_acc, max_all, total_all, delta_all = lax.fori_loop(
        0, count_heads, one_head, initial
    )
    cotangent_pair = jnp.stack((key_acc, value_acc))
    own_total = cotangent_pair[:, 0:group_len]
    for hop_count in range(1, PAST + 1):
        lower_row = hop_count * group_len
        own_total = pass_back(own_total, -1) + cotangent_pair[:, lower_row : lower_row + group_len]
    query_heads = query_acc.astype(jnp.bfloat16)
    key_heads = own_total[0].astype(jnp.bfloat16)
    value_heads = own_total[1].astype(jnp.bfloat16)
    token_q, token_k, token_v = (
        lax.all_to_all(query_heads, "seq", split_axis=0, concat_axis=1, tiled=True),
        lax.all_to_all(key_heads, "seq", split_axis=0, concat_axis=1, tiled=True),
        lax.all_to_all(value_heads, "seq", split_axis=0, concat_axis=1, tiled=True),
    )
    query_grad, query_terms = denormalize(q_values, q_inv, query_gain, token_q)
    key_grad, key_terms = denormalize(k_values, k_inv, key_gain, token_k)
    query_total, key_total_gain = lax.psum((query_terms, key_terms), ("group", "seq", "rep"))
    rep_width = feature_width // lax.axis_size("rep")
    offset = lax.axis_index("rep") * rep_width
    return (
        query_grad.reshape(query_raw.shape),
        key_grad.reshape(key_raw.shape),
        token_v.reshape(value_in.shape),
        lax.dynamic_slice_in_dim(query_total, offset, rep_width),
        lax.dynamic_slice_in_dim(key_total_gain, offset, rep_width),
    )


def body(*arrays):
    tokens, width = arrays[0].shape[2:]
    owners = lax.axis_size("group") * lax.axis_size("seq")
    heads = width // HEAD_DIM
    even = heads % owners == 0 and owners & (owners - 1) == 0 and owners % lax.axis_size("rep") == 0
    if even and tokens * owners * heads <= 32768 and tokens % 16 == 0 and tokens * owners >= heads * 8:
        return head_body(*arrays)
    return ring_body(*arrays)


def solution(mesh):
    placed = (
        P("rep", "group", "seq", None),
        P("rep", "group", "seq", None),
        P("rep", "group", "seq", None),
        P("rep", "group", "seq", None),
        P(),
        P(),
        P("rep", "group"),
    )
    return jax.shard_map(
        body,
        mesh=mesh,
        in_specs=placed,
        out_specs=(
            P("rep", "group", "seq", None),
            P("rep", "group", "seq", None),
            P("rep", "group", "seq", None),
            P("rep"),
            P("rep"),
        ),
        check_vma=False,
    )
```
